768 devices in a mesh: dp: 12 (over z), fsdp: 64 (over x, y, core).
Axes of the slice: x: 4, y: 8, z: 12, core: 2. Of those that a mesh axis runs over, the one named last changes fastest.
Arguments:
- grads: bfloat16 [12, 12, 512, 16, 1024], P('dp', None, 'fsdp'), may hold values from -50 to 50
- slot_block: int32 [12, 64], replicated, may hold values from 0 to 63, each once within a row
Outputs:
- update: bfloat16 [12, 512, 16, 1024], P('dp', 'fsdp')
- slot_roots: bfloat16 [12, 64, 2, 512, 512], P('dp', 'fsdp')
The draws below stay inside these ranges and needn't reach their ends.
Inputs may be any that keep to these rules, and one draw needn't show every extreme that they name: `slot_block`: row r is a permutation of 0 to 64 - 1 over the slots of the owners (owner o holds slots o * 1 to o + 1 - 1); a value v below 32 places local block v of index r of dp in that slot, a larger value leaves it empty.
All inputs are finite; a program needn't handle non-finite values.
Results may differ from the reference program's by a relative error of at most 0.033.
Values may be sent and summed in bfloat16 or wider, within the bound.
No kernel may reach another device: no remote copies, remote signals or barrier semaphores. Data moves between devices by JAX's collectives and lax.ppermute only.
A program may use at most 32 MiB of HBM per device.

```python
import math
import jax
import jax.numpy as jnp
from jax import lax

KV = 1024
BLK = 512
ITERS = 2
NMAT = 12
RB = 16
SLOTS = 64
N_DP = 12


def draw_grads(key, part):
    key = jax.random.fold_in(key, 11)
    subkeys = jax.random.split(key, 4)
    full_shape = (N_DP, NMAT, BLK, RB, KV)
    common = jax.random.normal(subkeys[0], (1, NMAT, BLK, RB, KV), jnp.float32)
    row_scale = jnp.exp(jax.random.uniform(subkeys[1], (1, 1, BLK, RB, 1), jnp.float32, 0.0, math.log(10.0)))
    col_scale = jnp.exp(jax.random.uniform(subkeys[2], (1, 1, 1, 1, KV), jnp.float32, 0.0, math.log(10.0)))
    replica = jnp.power(3.0, jnp.arange(N_DP, dtype=jnp.float32) / max(N_DP - 1, 1)).reshape(N_DP, 1, 1, 1, 1)
    independent = jax.random.normal(subkeys[3], full_shape, jnp.float32)
    values = (0.5 * common + independent) * row_scale * col_scale * replica / 20.0
    return jnp.clip(values, -50.0, 50.0).astype(jnp.bfloat16)


def setup_inputs(seed: int = 0) -> dict:
    keys = jax.random.split(jax.random.key(seed), 3)
    grads = draw_grads(jax.random.fold_in(keys[2], 71), 0)
    slot_block = jax.vmap(lambda own: jax.random.permutation(own, SLOTS))(jax.random.split(keys[1], N_DP)).reshape((N_DP, SLOTS)).astype(jnp.int32)
    return {"grads": grads, "slot_block": slot_block}


damping = 0.1

def left_gram(block_data):
    return jnp.dot(block_data, block_data.T, precision=lax.Precision.HIGHEST, preferred_element_type=jnp.float32)

def right_gram(block_data):
    return jnp.dot(block_data.T, block_data, precision=lax.Precision.HIGHEST, preferred_element_type=jnp.float32)

def stat_root(statistic):
    order = statistic.shape[0]
    identity = jnp.eye(order, dtype=jnp.float32)
    trace_sum = jnp.trace(statistic)
    damped = statistic + (damping * trace_sum / order + 1e-06) * identity
    norm_scale = jnp.sqrt(jnp.sum(damped * damped)) / 4.0
    matrix = damped / norm_scale
    root_iter = identity
    for iteration in range(ITERS):
        factor = (5.0 * identity - matrix) / 4.0
        factor_low = factor.astype(jnp.bfloat16)
        if iteration == 0:
            root_iter = jnp.power(norm_scale, -0.25) * factor
        else:
            root_iter = jnp.dot(root_iter.astype(jnp.bfloat16), factor_low, preferred_element_type=jnp.float32)
        if iteration + 1 < ITERS:
            square = jnp.dot(factor_low, factor_low, preferred_element_type=jnp.float32).astype(jnp.bfloat16)
            fourth = jnp.dot(square, square, preferred_element_type=jnp.float32).astype(jnp.bfloat16)
            matrix = jnp.dot(fourth, matrix.astype(jnp.bfloat16), preferred_element_type=jnp.float32)
    return root_iter.astype(jnp.bfloat16)

def graft_step(block_data, left_root, right_root):
    partial_product = jnp.dot(left_root, block_data.astype(jnp.bfloat16), preferred_element_type=jnp.float32).astype(jnp.bfloat16)
    direction = jnp.dot(partial_product, right_root, preferred_element_type=jnp.float32)
    grad_rms = jnp.sqrt(jnp.mean(block_data * block_data))
    dir_rms = jnp.sqrt(jnp.mean(direction * direction) + 1e-06)
    return (-(grad_rms / dir_rms) * direction).astype(jnp.bfloat16)

def precondition(block_data):
    left_root = stat_root(left_gram(block_data))
    right_root = stat_root(right_gram(block_data))
    return (jnp.stack([left_root, right_root]), graft_step(block_data, left_root, right_root))

def reference(grads, slot_block):
    averaged = lax.optimization_barrier(jnp.sum(grads, axis=0, dtype=jnp.float32)) / N_DP
    matrices, row_count, row_blocks, col_count = averaged.shape
    col_blocks = col_count // BLK
    tiles = averaged.reshape(matrices, row_count, row_blocks, col_blocks, BLK)
    tiles = tiles.transpose(0, 2, 3, 1, 4).reshape(matrices * row_blocks * col_blocks, row_count, BLK)
    root_pairs, updates = lax.map(precondition, tiles)
    update = updates.reshape(matrices, row_blocks, col_blocks, row_count, BLK)
    update = update.transpose(0, 3, 1, 2, 4).reshape(matrices, row_count, row_blocks, col_count)
    group_size = tiles.shape[0] // N_DP
    occupied = slot_block < group_size
    position = jnp.arange(N_DP, dtype=jnp.int32)[:, None] * group_size + jnp.minimum(slot_block, group_size - 1).astype(jnp.int32)
    slot_roots = jnp.take(root_pairs, position.reshape(-1), axis=0)
    slot_roots = slot_roots.reshape(N_DP, slot_block.shape[1], 2, BLK, BLK)
    slot_roots = jnp.where(occupied[:, :, None, None, None], slot_roots, jnp.zeros_like(slot_roots))
    return (update, slot_roots)
```

```python
import jax
import jax.numpy as jnp
from jax import lax
from jax.experimental import pallas as pl
from jax.experimental.pallas import tpu as pltpu
from jax.sharding import PartitionSpec as P

BLK = 512
LANES = 128
PER_BLK = BLK // LANES
ITERS = 2
DAMPING = 0.1
F32 = jnp.float32
BF16 = jnp.bfloat16
VMEM_LIMIT = 48 * 1024 * 1024


def cost(flops, nbytes):
    return pl.CostEstimate(flops=flops, bytes_accessed=nbytes, transcendentals=0)


def vmem():
    return pl.BlockSpec(memory_space=pltpu.VMEM)


def smem():
    return pl.BlockSpec(memory_space=pltpu.SMEM)


def params():
    return pltpu.CompilerParams(vmem_limit_bytes=VMEM_LIMIT)


def outgoing_pieces(table, summed):
    rows, row_blocks, cols = summed.shape
    col_blocks = cols // BLK
    group = row_blocks * col_blocks
    slots = table.shape[0]

    def kernel(table_ref, x_ref, out_ref, wide, pieces):
        for k in range(cols // LANES):
            lanes = x_ref[:, :, k * LANES : (k + 1) * LANES].astype(F32)
            wide[k] = lanes.reshape(rows * row_blocks, LANES)
        for rb in range(row_blocks):
            for k in range(cols // LANES):
                v, at = rb * col_blocks + k // PER_BLK, k % PER_BLK * LANES
                part = wide[k, pl.ds(rb, rows, stride=row_blocks), :]
                pieces[v, :, at : at + LANES] = part.astype(BF16)
        pieces[group:] = jnp.zeros((slots - group, rows, BLK), BF16)

        def place(s, carry):
            out_ref[s] = pieces[table_ref[s]]
            return carry

        lax.fori_loop(0, slots, place, 0, unroll=8)

    return pl.pallas_call(
        kernel,
        out_shape=jax.ShapeDtypeStruct((slots, rows, BLK), BF16),
        in_specs=[smem(), vmem()],
        out_specs=vmem(),
        scratch_shapes=[
            pltpu.VMEM((cols // LANES, rows * row_blocks, LANES), F32),
            pltpu.VMEM((slots, rows, BLK), BF16),
        ],
        compiler_params=params(),
        cost_estimate=cost(0, 3 * slots * rows * BLK * 2),
        name="outgoing",
    )(table, summed)


def incoming_update(table, returned, row_blocks, col_blocks):
    slots, rows, _ = returned.shape
    cols = col_blocks * BLK

    def kernel(table_ref, x_ref, out_ref, wide, pieces):
        def place(s, carry):
            pieces[table_ref[s]] = x_ref[s]
            return carry

        lax.fori_loop(0, slots, place, 0, unroll=8)
        for rb in range(row_blocks):
            for k in range(cols // LANES):
                v, at = rb * col_blocks + k // PER_BLK, k % PER_BLK * LANES
                part = pieces[v, :, at : at + LANES].astype(F32)
                wide[k, pl.ds(rb, rows, stride=row_blocks), :] = part
        for k in range(cols // LANES):
            lanes = wide[k].reshape(rows, row_blocks, LANES)
            out_ref[:, :, k * LANES : (k + 1) * LANES] = lanes.astype(BF16)

    return pl.pallas_call(
        kernel,
        out_shape=jax.ShapeDtypeStruct((rows, row_blocks, cols), BF16),
        in_specs=[smem(), vmem()],
        out_specs=vmem(),
        scratch_shapes=[
            pltpu.VMEM((cols // LANES, rows * row_blocks, LANES), F32),
            pltpu.VMEM((slots, rows, BLK), BF16),
        ],
        compiler_params=params(),
        cost_estimate=cost(0, 3 * slots * rows * BLK * 2),
        name="incoming",
    )(table, returned)


def dot(a, b, contract=((1,), (0,))):
    return lax.dot_general(a, b, (contract, ((), ())), preferred_element_type=F32)


def newton_root(stat, total, eye):
    damped = stat + (DAMPING * total / BLK + 1e-06) * eye
    scale = jnp.sqrt(jnp.sum(damped * damped)) / 4.0
    matrix = damped * (1.0 / scale)
    root = None
    for iteration in range(ITERS):
        factor = 1.25 * eye - 0.25 * matrix
        factor_low = factor.astype(BF16)
        if iteration == 0:
            root = (lax.rsqrt(jnp.sqrt(scale)) * factor).astype(BF16)
        else:
            root = dot(root, factor_low).astype(BF16)
        if iteration + 1 < ITERS:
            square = dot(factor_low, factor_low).astype(BF16)
            fourth = dot(square, square).astype(BF16)
            matrix = dot(fourth, matrix.astype(BF16))
    return root


def owner_work(active, block, replicas):
    def kernel(active_ref, x_ref, roots_ref, update_ref):
        @pl.when(active_ref[0] == 0)
        def _():
            roots_ref[...] = jnp.zeros_like(roots_ref)
            update_ref[...] = jnp.zeros_like(update_ref)

        @pl.when(active_ref[0] != 0)
        def _():
            eye = (
                lax.broadcasted_iota(jnp.int32, (BLK, BLK), 0)
                == lax.broadcasted_iota(jnp.int32, (BLK, BLK), 1)
            ).astype(F32)
            x = x_ref[...]
            wide = x.astype(F32)
            scale = 1.0 / (replicas * replicas)
            total = jnp.sum(wide * wide) * scale
            left = newton_root(dot(x, x, ((1,), (1,))) * scale, total, eye)
            roots_ref[0] = left
            right = newton_root(dot(x, x, ((0,), (0,))) * scale, total, eye)
            roots_ref[1] = right
            partial = (dot(left, x) * (1.0 / replicas)).astype(BF16)
            direction = dot(partial, right)
            count = BLK * BLK
            grad_rms = jnp.sqrt(total / count)
            dir_rms = jnp.sqrt(jnp.sum(direction * direction) / count + 1e-06)
            update_ref[...] = (-(grad_rms / dir_rms) * direction).astype(BF16)

    return pl.pallas_call(
        kernel,
        out_shape=(
            jax.ShapeDtypeStruct((2, BLK, BLK), BF16),
            jax.ShapeDtypeStruct((BLK, BLK), BF16),
        ),
        in_specs=[smem(), vmem()],
        out_specs=(vmem(), vmem()),
        compiler_params=params(),
        cost_estimate=cost(24 * BLK**3, 8 * BLK * BLK),
        name="owner",
    )(active, block)


def local(grads, slot_block):
    replicas = lax.axis_size("dp")
    table = lax.dynamic_index_in_dim(slot_block, lax.axis_index("dp"), 0, keepdims=False)
    slots = table.shape[0]
    summed = lax.psum_scatter(grads[0], "dp", scatter_dimension=0, tiled=True)[0]
    rows, row_blocks, cols = summed.shape
    col_blocks = cols // BLK
    group = row_blocks * col_blocks
    active = lax.dynamic_slice_in_dim(table, lax.axis_index("fsdp"), 1, 0) < group
    pieces = outgoing_pieces(table, summed)
    received = lax.all_to_all(pieces, "fsdp", split_axis=0, concat_axis=0, tiled=True)
    roots, update = owner_work(active.astype(jnp.int32), received.reshape(BLK, BLK), replicas)
    returned = lax.all_to_all(
        update.reshape(slots, rows, BLK), "fsdp", split_axis=0, concat_axis=0, tiled=True
    )
    result = incoming_update(table, returned, row_blocks, col_blocks)
    return result[None], roots[None, None]


def solution(mesh):
    return jax.shard_map(
        local,
        mesh=mesh,
        in_specs=(P("dp", None, "fsdp", None, None), P()),
        out_specs=(P("dp", "fsdp", None, None), P("dp", "fsdp", None, None, None)),
        check_vma=False,
    )
```

```python
import jax
import jax.numpy as jnp
from jax import lax
from jax.experimental import pallas as pl
from jax.experimental.pallas import tpu as pltpu
from jax.sharding import PartitionSpec as P

BLK = 512
LANES = 128
PER_BLK = BLK // LANES
ITERS = 2
DAMPING = 0.1
F32 = jnp.float32
BF16 = jnp.bfloat16
VMEM_LIMIT = 48 * 1024 * 1024


def cost(flops, nbytes):
    return pl.CostEstimate(flops=flops, bytes_accessed=nbytes, transcendentals=0)


def vmem():
    return pl.BlockSpec(memory_space=pltpu.VMEM)


def smem():
    return pl.BlockSpec(memory_space=pltpu.SMEM)


def params():
    return pltpu.CompilerParams(vmem_limit_bytes=VMEM_LIMIT)


def outgoing_pieces(table, terms):
    rows, row_blocks, cols = terms[0].shape
    col_blocks = cols // BLK
    group = row_blocks * col_blocks
    slots = table.shape[0]

    def kernel(table_ref, *refs):
        x_refs, (out_ref, wide, pieces) = refs[: len(terms)], refs[len(terms) :]
        for k in range(cols // LANES):
            lanes = sum(x[:, :, k * LANES : (k + 1) * LANES].astype(F32) for x in x_refs)
            wide[k] = lanes.reshape(rows * row_blocks, LANES)
        for rb in range(row_blocks):
            for k in range(cols // LANES):
                v, at = rb * col_blocks + k // PER_BLK, k % PER_BLK * LANES
                part = wide[k, pl.ds(rb, rows, stride=row_blocks), :]
                pieces[v, :, at : at + LANES] = part.astype(BF16)
        pieces[group:] = jnp.zeros((slots - group, rows, BLK), BF16)

        def place(s, carry):
            out_ref[s] = pieces[table_ref[s]]
            return carry

        lax.fori_loop(0, slots, place, 0, unroll=8)

    return pl.pallas_call(
        kernel,
        out_shape=jax.ShapeDtypeStruct((slots, rows, BLK), BF16),
        in_specs=[smem()] + [vmem()] * len(terms),
        out_specs=vmem(),
        scratch_shapes=[
            pltpu.VMEM((cols // LANES, rows * row_blocks, LANES), F32),
            pltpu.VMEM((slots, rows, BLK), BF16),
        ],
        compiler_params=params(),
        cost_estimate=cost(0, 3 * slots * rows * BLK * 2),
        name="outgoing",
    )(table, *terms)


def incoming_update(table, returned, row_blocks, col_blocks):
    slots, rows, _ = returned.shape
    cols = col_blocks * BLK

    def kernel(table_ref, x_ref, out_ref, wide, pieces):
        def place(s, carry):
            pieces[table_ref[s]] = x_ref[s]
            return carry

        lax.fori_loop(0, slots, place, 0, unroll=8)
        for rb in range(row_blocks):
            for k in range(cols // LANES):
                v, at = rb * col_blocks + k // PER_BLK, k % PER_BLK * LANES
                part = pieces[v, :, at : at + LANES].astype(F32)
                wide[k, pl.ds(rb, rows, stride=row_blocks), :] = part
        for k in range(cols // LANES):
            lanes = wide[k].reshape(rows, row_blocks, LANES)
            out_ref[:, :, k * LANES : (k + 1) * LANES] = lanes.astype(BF16)

    return pl.pallas_call(
        kernel,
        out_shape=jax.ShapeDtypeStruct((rows, row_blocks, cols), BF16),
        in_specs=[smem(), vmem()],
        out_specs=vmem(),
        scratch_shapes=[
            pltpu.VMEM((cols // LANES, rows * row_blocks, LANES), F32),
            pltpu.VMEM((slots, rows, BLK), BF16),
        ],
        compiler_params=params(),
        cost_estimate=cost(0, 3 * slots * rows * BLK * 2),
        name="incoming",
    )(table, returned)


def dot(a, b, contract=((1,), (0,))):
    return lax.dot_general(a, b, (contract, ((), ())), preferred_element_type=F32)


def newton_root(stat, total, eye):
    damped = stat + (DAMPING * total / BLK + 1e-06) * eye
    scale = jnp.sqrt(jnp.sum(damped * damped)) / 4.0
    matrix = damped * (1.0 / scale)
    root = None
    for iteration in range(ITERS):
        factor = 1.25 * eye - 0.25 * matrix
        factor_low = factor.astype(BF16)
        if iteration == 0:
            root = (lax.rsqrt(jnp.sqrt(scale)) * factor).astype(BF16)
        else:
            root = dot(root, factor_low).astype(BF16)
        if iteration + 1 < ITERS:
            square = dot(factor_low, factor_low).astype(BF16)
            fourth = dot(square, square).astype(BF16)
            matrix = dot(fourth, matrix.astype(BF16))
    return root


def owner_work(active, block, replicas):
    def kernel(active_ref, x_ref, roots_ref, update_ref):
        @pl.when(active_ref[0] == 0)
        def _():
            roots_ref[...] = jnp.zeros_like(roots_ref)
            update_ref[...] = jnp.zeros_like(update_ref)

        @pl.when(active_ref[0] != 0)
        def _():
            eye = (
                lax.broadcasted_iota(jnp.int32, (BLK, BLK), 0)
                == lax.broadcasted_iota(jnp.int32, (BLK, BLK), 1)
            ).astype(F32)
            x = x_ref[...]
            wide = x.astype(F32)
            scale = 1.0 / (replicas * replicas)
            total = jnp.sum(wide * wide) * scale
            left = newton_root(dot(x, x, ((1,), (1,))) * scale, total, eye)
            roots_ref[0] = left
            right = newton_root(dot(x, x, ((0,), (0,))) * scale, total, eye)
            roots_ref[1] = right
            partial = (dot(left, x) * (1.0 / replicas)).astype(BF16)
            direction = dot(partial, right)
            count = BLK * BLK
            grad_rms = jnp.sqrt(total / count)
            dir_rms = jnp.sqrt(jnp.sum(direction * direction) / count + 1e-06)
            update_ref[...] = (-(grad_rms / dir_rms) * direction).astype(BF16)

    return pl.pallas_call(
        kernel,
        out_shape=(
            jax.ShapeDtypeStruct((2, BLK, BLK), BF16),
            jax.ShapeDtypeStruct((BLK, BLK), BF16),
        ),
        in_specs=[smem(), vmem()],
        out_specs=(vmem(), vmem()),
        compiler_params=params(),
        cost_estimate=cost(24 * BLK**3, 8 * BLK * BLK),
        name="owner",
    )(active, block)


def ring_terms(parts, axis):
    n = parts.shape[0]
    here = lax.axis_index(axis)
    raising = [(i, (i + 1) % n) for i in range(n)]
    lowering = [(i, (i - 1) % n) for i in range(n)]
    hops = n // 2

    def own(offset):
        return lax.dynamic_index_in_dim(parts, (here + offset + n) % n, 0, keepdims=False)

    def plus(total, offset):
        if total is None:
            return own(offset)
        return (total.astype(F32) + own(offset).astype(F32)).astype(BF16)

    below = above = None
    for step in range(hops):
        below = lax.ppermute(plus(below, hops - step), axis, raising)
        if step >= 2 * hops + 1 - n:
            above = lax.ppermute(plus(above, step - hops), axis, lowering)
    return below, above, own(0)


def local(grads, slot_block):
    replicas = lax.axis_size("dp")
    table = lax.dynamic_index_in_dim(slot_block, lax.axis_index("dp"), 0, keepdims=False)
    slots = table.shape[0]
    terms = ring_terms(grads[0], "dp")
    rows, row_blocks, cols = terms[0].shape
    col_blocks = cols // BLK
    group = row_blocks * col_blocks
    active = lax.dynamic_slice_in_dim(table, lax.axis_index("fsdp"), 1, 0) < group
    pieces = outgoing_pieces(table, terms)
    received = lax.all_to_all(pieces, "fsdp", split_axis=0, concat_axis=0, tiled=True)
    roots, update = owner_work(active.astype(jnp.int32), received.reshape(BLK, BLK), replicas)
    returned = lax.all_to_all(
        update.reshape(slots, rows, BLK), "fsdp", split_axis=0, concat_axis=0, tiled=True
    )
    result = incoming_update(table, returned, row_blocks, col_blocks)
    return result[None], roots[None, None]


def solution(mesh):
    return jax.shard_map(
        local,
        mesh=mesh,
        in_specs=(P("dp", None, "fsdp", None, None), P()),
        out_specs=(P("dp", "fsdp", None, None), P("dp", "fsdp", None, None, None)),
        check_vma=False,
    )
```

```python
import jax
import jax.numpy as jnp
from jax import lax
from jax.experimental import pallas as pl
from jax.experimental.pallas import tpu as pltpu
from jax.sharding import PartitionSpec as P

BLK = 512
LANES = 128
PER_BLK = BLK // LANES
ITERS = 2
DAMPING = 0.1
F32 = jnp.float32
BF16 = jnp.bfloat16
VMEM_LIMIT = 24 * 1024 * 1024


def cost(flops, nbytes):
    return pl.CostEstimate(flops=flops, bytes_accessed=nbytes, transcendentals=0)


def vmem():
    return pl.BlockSpec(memory_space=pltpu.VMEM)


def smem():
    return pl.BlockSpec(memory_space=pltpu.SMEM)


def params():
    return pltpu.CompilerParams(vmem_limit_bytes=VMEM_LIMIT)


def outgoing_pieces(here, table, terms, parts):
    rows, row_blocks, cols = terms[0].shape
    col_blocks = cols // BLK
    group = row_blocks * col_blocks
    slots = table.shape[0]

    def kernel(here_ref, table_ref, below_ref, above_ref, parts_ref, out_ref, wide, pieces):
        for k in range(cols // LANES):
            at = (slice(None), slice(None), slice(k * LANES, (k + 1) * LANES))
            lanes = below_ref[at].astype(F32) + above_ref[at].astype(F32)
            lanes = lanes + parts_ref[(here_ref[0], *at)].astype(F32)
            wide[k] = lanes.reshape(rows * row_blocks, LANES)
        for rb in range(row_blocks):
            for k in range(cols // LANES):
                v, at = rb * col_blocks + k // PER_BLK, k % PER_BLK * LANES
                part = wide[k, pl.ds(rb, rows, stride=row_blocks), :]
                pieces[v, :, at : at + LANES] = part.astype(BF16)
        pieces[group:] = jnp.zeros((slots - group, rows, BLK), BF16)

        def place(s, carry):
            out_ref[s] = pieces[table_ref[s]]
            return carry

        lax.fori_loop(0, slots, place, 0, unroll=8)

    return pl.pallas_call(
        kernel,
        out_shape=jax.ShapeDtypeStruct((slots, rows, BLK), BF16),
        in_specs=[smem(), smem(), vmem(), vmem(), vmem()],
        out_specs=vmem(),
        scratch_shapes=[
            pltpu.VMEM((cols // LANES, rows * row_blocks, LANES), F32),
            pltpu.VMEM((slots, rows, BLK), BF16),
        ],
        compiler_params=params(),
        cost_estimate=cost(0, 3 * slots * rows * BLK * 2),
        name="outgoing",
    )(here, table, *terms, parts)


def incoming_update(table, returned, row_blocks, col_blocks):
    slots, rows, _ = returned.shape
    cols = col_blocks * BLK

    def kernel(table_ref, x_ref, out_ref, wide, pieces):
        def place(s, carry):
            pieces[table_ref[s]] = x_ref[s]
            return carry

        lax.fori_loop(0, slots, place, 0, unroll=8)
        for rb in range(row_blocks):
            for k in range(cols // LANES):
                v, at = rb * col_blocks + k // PER_BLK, k % PER_BLK * LANES
                part = pieces[v, :, at : at + LANES].astype(F32)
                wide[k, pl.ds(rb, rows, stride=row_blocks), :] = part
        for k in range(cols // LANES):
            lanes = wide[k].reshape(rows, row_blocks, LANES)
            out_ref[:, :, k * LANES : (k + 1) * LANES] = lanes.astype(BF16)

    return pl.pallas_call(
        kernel,
        out_shape=jax.ShapeDtypeStruct((rows, row_blocks, cols), BF16),
        in_specs=[smem(), vmem()],
        out_specs=vmem(),
        scratch_shapes=[
            pltpu.VMEM((cols // LANES, rows * row_blocks, LANES), F32),
            pltpu.VMEM((slots, rows, BLK), BF16),
        ],
        compiler_params=params(),
        cost_estimate=cost(0, 3 * slots * rows * BLK * 2),
        name="incoming",
    )(table, returned)


def dot(a, b, contract=((1,), (0,))):
    return lax.dot_general(a, b, (contract, ((), ())), preferred_element_type=F32)


def newton_root(stat, total, eye):
    damped = stat + (DAMPING * total / BLK + 1e-06) * eye
    scale = jnp.sqrt(jnp.sum(damped * damped)) / 4.0
    matrix = damped * (1.0 / scale)
    root = None
    for iteration in range(ITERS):
        factor = 1.25 * eye - 0.25 * matrix
        factor_low = factor.astype(BF16)
        if iteration == 0:
            root = (lax.rsqrt(jnp.sqrt(scale)) * factor).astype(BF16)
        else:
            root = dot(root, factor_low).astype(BF16)
        if iteration + 1 < ITERS:
            square = dot(factor_low, factor_low).astype(BF16)
            fourth = dot(square, square).astype(BF16)
            matrix = dot(fourth, matrix.astype(BF16))
    return root


def owner_work(active, block, replicas):
    def kernel(active_ref, x_ref, roots_ref, update_ref):
        @pl.when(active_ref[0] == 0)
        def _():
            roots_ref[...] = jnp.zeros_like(roots_ref)
            update_ref[...] = jnp.zeros_like(update_ref)

        @pl.when(active_ref[0] != 0)
        def _():
            eye = (
                lax.broadcasted_iota(jnp.int32, (BLK, BLK), 0)
                == lax.broadcasted_iota(jnp.int32, (BLK, BLK), 1)
            ).astype(F32)
            x = x_ref[...]
            wide = x.astype(F32)
            scale = 1.0 / (replicas * replicas)
            total = jnp.sum(wide * wide) * scale
            left = newton_root(dot(x, x, ((1,), (1,))) * scale, total, eye)
            roots_ref[0] = left
            right = newton_root(dot(x, x, ((0,), (0,))) * scale, total, eye)
            roots_ref[1] = right
            partial = (dot(left, x) * (1.0 / replicas)).astype(BF16)
            direction = dot(partial, right)
            count = BLK * BLK
            grad_rms = jnp.sqrt(total / count)
            dir_rms = jnp.sqrt(jnp.sum(direction * direction) / count + 1e-06)
            update_ref[...] = (-(grad_rms / dir_rms) * direction).astype(BF16)

    return pl.pallas_call(
        kernel,
        out_shape=(
            jax.ShapeDtypeStruct((2, BLK, BLK), BF16),
            jax.ShapeDtypeStruct((BLK, BLK), BF16),
        ),
        in_specs=[smem(), vmem()],
        out_specs=(vmem(), vmem()),
        compiler_params=params(),
        cost_estimate=cost(24 * BLK**3, 8 * BLK * BLK),
        name="owner",
    )(active, block)


def part_at(parts_ref, here_ref, offset):
    return parts_ref[lax.rem(here_ref[0] + offset, parts_ref.shape[0])]


def picked(here, parts, offsets):
    def kernel(here_ref, parts_ref, *out_refs):
        for offset, out_ref in zip(offsets, out_refs):
            out_ref[...] = part_at(parts_ref, here_ref, offset)

    return pl.pallas_call(
        kernel,
        out_shape=[jax.ShapeDtypeStruct(parts.shape[1:], BF16)] * len(offsets),
        in_specs=[smem(), vmem()],
        out_specs=[vmem()] * len(offsets),
        compiler_params=params(),
        cost_estimate=cost(0, 4 * parts[0].size * len(offsets)),
        name="picked",
    )(here, parts)


def added(here, total, parts, offset):
    def kernel(here_ref, total_ref, parts_ref, out_ref):
        own = part_at(parts_ref, here_ref, offset).astype(F32)
        out_ref[...] = (total_ref[...].astype(F32) + own).astype(BF16)

    return pl.pallas_call(
        kernel,
        out_shape=jax.ShapeDtypeStruct(total.shape, BF16),
        in_specs=[smem(), vmem(), vmem()],
        out_specs=vmem(),
        compiler_params=params(),
        cost_estimate=cost(total.size, 6 * total.size),
        name="added",
    )(here, total, parts)


def ring_terms(here, parts, axis):
    n = parts.shape[0]
    raising = [(i, (i + 1) % n) for i in range(n)]
    lowering = [(i, (i - 1) % n) for i in range(n)]
    hops = n // 2
    first = 2 * hops + 1 - n
    below, above = picked(here, parts, (hops, (first - hops) % n))
    for step in range(hops):
        if step > 0:
            below = added(here, below, parts, hops - step)
        below = lax.ppermute(below, axis, raising)
        if step > first:
            above = added(here, above, parts, (step - hops) % n)
        if step >= first:
            above = lax.ppermute(above, axis, lowering)
    return below, above


def local(grads, slot_block):
    replicas = lax.axis_size("dp")
    table = lax.dynamic_index_in_dim(slot_block, lax.axis_index("dp"), 0, keepdims=False)
    slots = table.shape[0]
    here = lax.axis_index("dp")[None]
    terms = ring_terms(here, grads[0], "dp")
    rows, row_blocks, cols = terms[0].shape
    col_blocks = cols // BLK
    group = row_blocks * col_blocks
    active = lax.dynamic_slice_in_dim(table, lax.axis_index("fsdp"), 1, 0) < group
    pieces = outgoing_pieces(here, table, terms, grads[0])
    received = lax.all_to_all(pieces, "fsdp", split_axis=0, concat_axis=0, tiled=True)
    roots, update = owner_work(active.astype(jnp.int32), received.reshape(BLK, BLK), replicas)
    returned = lax.all_to_all(
        update.reshape(slots, rows, BLK), "fsdp", split_axis=0, concat_axis=0, tiled=True
    )
    result = incoming_update(table, returned, row_blocks, col_blocks)
    return result[None], roots[None, None]


def solution(mesh):
    return jax.shard_map(
        local,
        mesh=mesh,
        in_specs=(P("dp", None, "fsdp", None, None), P()),
        out_specs=(P("dp", "fsdp", None, None), P("dp", "fsdp", None, None, None)),
        check_vma=False,
    )
```

```python
import jax
import jax.numpy as jnp
from jax import lax
from jax.experimental import pallas as pl
from jax.experimental.pallas import tpu as pltpu
from jax.sharding import PartitionSpec as P

BLK = 512
LANES = 128
PER_BLK = BLK // LANES
ITERS = 2
DAMPING = 0.1
F32 = jnp.float32
BF16 = jnp.bfloat16
VMEM_LIMIT = 24 * 1024 * 1024


def cost(flops, nbytes):
    return pl.CostEstimate(flops=flops, bytes_accessed=nbytes, transcendentals=0)


def vmem():
    return pl.BlockSpec(memory_space=pltpu.VMEM)


def smem():
    return pl.BlockSpec(memory_space=pltpu.SMEM)


def params():
    return pltpu.CompilerParams(vmem_limit_bytes=VMEM_LIMIT)


def assigned(table):
    slots = table.shape[0]
    chips = slots // 2

    def kernel(table_ref, first_ref, second_ref, spare):
        def collect(p, count):
            low, high = table_ref[2 * p], table_ref[2 * p + 1]
            two = jnp.logical_and(low < chips, high < chips)
            first_ref[p] = jnp.minimum(jnp.where(low < chips, low, high), chips)
            second_ref[p] = jnp.where(two, high, chips)
            spare[count] = high
            return count + two.astype(jnp.int32)

        def fill(p, count):
            empty = first_ref[p] == chips
            first_ref[p] = jnp.where(empty, spare[count], first_ref[p])
            return count + empty.astype(jnp.int32)

        lax.fori_loop(0, chips, collect, jnp.int32(0))
        lax.fori_loop(0, chips, fill, jnp.int32(0))

    return pl.pallas_call(
        kernel,
        out_shape=[jax.ShapeDtypeStruct((chips,), jnp.int32)] * 2,
        in_specs=[smem()],
        out_specs=[smem(), smem()],
        scratch_shapes=[pltpu.SMEM((chips + 1,), jnp.int32)],
        compiler_params=params(),
        cost_estimate=cost(0, 1024),
        name="assigned",
    )(table)


def outgoing_pieces(here, first, second, terms, parts):
    rows, row_blocks, cols = terms[0].shape
    col_blocks = cols // BLK
    group = row_blocks * col_blocks
    chips = first.shape[0]

    def kernel(
        here_ref, first_ref, second_ref, below_ref, above_ref, parts_ref, one_ref, two_ref, wide, pieces
    ):
        for k in range(cols // LANES):
            at = (slice(None), slice(None), slice(k * LANES, (k + 1) * LANES))
            lanes = below_ref[at].astype(F32) + above_ref[at].astype(F32)
            lanes = lanes + parts_ref[(here_ref[0], *at)].astype(F32)
            wide[k] = lanes.reshape(rows * row_blocks, LANES)
        for rb in range(row_blocks):
            for k in range(cols // LANES):
                v, at = rb * col_blocks + k // PER_BLK, k % PER_BLK * LANES
                part = wide[k, pl.ds(rb, rows, stride=row_blocks), :]
                pieces[v, :, at : at + LANES] = part.astype(BF16)
        pieces[group] = jnp.zeros((rows, BLK), BF16)

        def place(p, carry):
            one_ref[p] = pieces[first_ref[p]]
            two_ref[p] = pieces[second_ref[p]]
            return carry

        lax.fori_loop(0, chips, place, 0, unroll=4)

    return pl.pallas_call(
        kernel,
        out_shape=[jax.ShapeDtypeStruct((chips, rows, BLK), BF16)] * 2,
        in_specs=[smem(), smem(), smem(), vmem(), vmem(), vmem()],
        out_specs=[vmem(), vmem()],
        scratch_shapes=[
            pltpu.VMEM((cols // LANES, rows * row_blocks, LANES), F32),
            pltpu.VMEM((group + 1, rows, BLK), BF16),
        ],
        compiler_params=params(),
        cost_estimate=cost(0, 6 * chips * rows * BLK * 2),
        name="outgoing",
    )(here, first, second, *terms, parts)


def incoming_update(first, returned, row_blocks, col_blocks):
    chips, rows, _ = returned.shape
    cols = col_blocks * BLK

    def kernel(first_ref, x_ref, out_ref, wide, pieces):
        def place(s, carry):
            pieces[first_ref[s]] = x_ref[s]
            return carry

        lax.fori_loop(0, chips, place, 0, unroll=4)
        for rb in range(row_blocks):
            for k in range(cols // LANES):
                v, at = rb * col_blocks + k // PER_BLK, k % PER_BLK * LANES
                part = pieces[v, :, at : at + LANES].astype(F32)
                wide[k, pl.ds(rb, rows, stride=row_blocks), :] = part
        for k in range(cols // LANES):
            lanes = wide[k].reshape(rows, row_blocks, LANES)
            out_ref[:, :, k * LANES : (k + 1) * LANES] = lanes.astype(BF16)

    return pl.pallas_call(
        kernel,
        out_shape=jax.ShapeDtypeStruct((rows, row_blocks, cols), BF16),
        in_specs=[smem(), vmem()],
        out_specs=vmem(),
        scratch_shapes=[
            pltpu.VMEM((cols // LANES, rows * row_blocks, LANES), F32),
            pltpu.VMEM((chips, rows, BLK), BF16),
        ],
        compiler_params=params(),
        cost_estimate=cost(0, 3 * chips * rows * BLK * 2),
        name="incoming",
    )(first, returned)


def dot(a, b, contract=((1,), (0,))):
    return lax.dot_general(a, b, (contract, ((), ())), preferred_element_type=F32)


def newton_root(stat, total, eye):
    damped = stat + (DAMPING * total / BLK + 1e-06) * eye
    scale = jnp.sqrt(jnp.sum(damped * damped)) / 4.0
    matrix = damped * (1.0 / scale)
    root = None
    for iteration in range(ITERS):
        factor = 1.25 * eye - 0.25 * matrix
        factor_low = factor.astype(BF16)
        if iteration == 0:
            root = (lax.rsqrt(jnp.sqrt(scale)) * factor).astype(BF16)
        else:
            root = dot(root, factor_low).astype(BF16)
        if iteration + 1 < ITERS:
            square = dot(factor_low, factor_low).astype(BF16)
            fourth = dot(square, square).astype(BF16)
            matrix = dot(fourth, matrix.astype(BF16))
    return root


def whole_block(core_ref, mine_ref, other_ref, halves):
    halves[:, core_ref[0]] = mine_ref[...].astype(F32)
    halves[:, 1 - core_ref[0]] = other_ref[...].astype(F32)
    return halves[...].reshape(BLK, BLK)


def both_roots(wide, replicas):
    eye = (
        lax.broadcasted_iota(jnp.int32, (BLK, BLK), 0)
        == lax.broadcasted_iota(jnp.int32, (BLK, BLK), 1)
    ).astype(F32)
    x = wide.astype(BF16)
    scale = 1.0 / (replicas * replicas)
    total = jnp.sum(wide * wide) * scale
    left = newton_root(dot(x, x, ((1,), (1,))) * scale, total, eye)
    right = newton_root(dot(x, x, ((0,), (0,))) * scale, total, eye)
    return x, total, left, right


def first_work(core, mine, other, replicas):
    chips, rows, _ = mine.shape

    def kernel(core_ref, mine_ref, other_ref, roots_ref, update_ref, halves):
        wide = whole_block(core_ref, mine_ref, other_ref, halves)
        x, total, left, right = both_roots(wide, replicas)
        roots_ref[0] = left
        roots_ref[1] = right
        partial = (dot(left, x) * (1.0 / replicas)).astype(BF16)
        direction = dot(partial, right)
        count = BLK * BLK
        grad_rms = jnp.sqrt(total / count)
        dir_rms = jnp.sqrt(jnp.sum(direction * direction) / count + 1e-06)
        halves[...] = (-(grad_rms / dir_rms) * direction).reshape(chips, 2, rows, BLK)
        update_ref[...] = halves[:, core_ref[0]].astype(BF16)

    return pl.pallas_call(
        kernel,
        out_shape=(
            jax.ShapeDtypeStruct((2, BLK, BLK), BF16),
            jax.ShapeDtypeStruct((chips, rows, BLK), BF16),
        ),
        in_specs=[smem(), vmem(), vmem()],
        out_specs=(vmem(), vmem()),
        scratch_shapes=[pltpu.VMEM((chips, 2, rows, BLK), F32)],
        compiler_params=params(),
        cost_estimate=cost(24 * BLK**3, 8 * BLK * BLK),
        name="first_work",
    )(core, mine, other)


def second_work(mode, core, mine, other, roots, replicas):
    chips, rows, _ = mine.shape

    def kernel(mode_ref, core_ref, mine_ref, other_ref, roots_ref, out_ref, halves):
        @pl.when(mode_ref[0] == 0)
        def _():
            out_ref[...] = jnp.zeros_like(out_ref)

        @pl.when(mode_ref[0] == 1)
        def _():
            out_ref[...] = roots_ref[...]

        @pl.when(mode_ref[0] == 2)
        def _():
            wide = whole_block(core_ref, mine_ref, other_ref, halves)
            _, _, left, right = both_roots(wide, replicas)
            out_ref[0] = left
            out_ref[1] = right

    return pl.pallas_call(
        kernel,
        out_shape=jax.ShapeDtypeStruct((2, BLK, BLK), BF16),
        in_specs=[smem(), smem(), vmem(), vmem(), vmem()],
        out_specs=vmem(),
        scratch_shapes=[pltpu.VMEM((chips, 2, rows, BLK), F32)],
        compiler_params=params(),
        cost_estimate=cost(20 * BLK**3, 8 * BLK * BLK),
        name="second_work",
    )(mode, core, mine, other, roots)


def part_at(parts_ref, here_ref, offset):
    return parts_ref[lax.rem(here_ref[0] + offset, parts_ref.shape[0])]


def picked(here, parts, offsets):
    def kernel(here_ref, parts_ref, *out_refs):
        for offset, out_ref in zip(offsets, out_refs):
            out_ref[...] = part_at(parts_ref, here_ref, offset)

    return pl.pallas_call(
        kernel,
        out_shape=[jax.ShapeDtypeStruct(parts.shape[1:], BF16)] * len(offsets),
        in_specs=[smem(), vmem()],
        out_specs=[vmem()] * len(offsets),
        compiler_params=params(),
        cost_estimate=cost(0, 4 * parts[0].size * len(offsets)),
        name="picked",
    )(here, parts)


def added(here, total, parts, offset):
    def kernel(here_ref, total_ref, parts_ref, out_ref):
        own = part_at(parts_ref, here_ref, offset).astype(F32)
        out_ref[...] = (total_ref[...].astype(F32) + own).astype(BF16)

    return pl.pallas_call(
        kernel,
        out_shape=jax.ShapeDtypeStruct(total.shape, BF16),
        in_specs=[smem(), vmem(), vmem()],
        out_specs=vmem(),
        compiler_params=params(),
        cost_estimate=cost(total.size, 6 * total.size),
        name="added",
    )(here, total, parts)


def ring_terms(here, parts, axis):
    n = parts.shape[0]
    raising = [(i, (i + 1) % n) for i in range(n)]
    lowering = [(i, (i - 1) % n) for i in range(n)]
    hops = n // 2
    first = 2 * hops + 1 - n
    below, above = picked(here, parts, (hops, (first - hops) % n))
    for step in range(hops):
        if step > 0:
            below = added(here, below, parts, hops - step)
        below = lax.ppermute(below, axis, raising)
        if step > first:
            above = added(here, above, parts, (step - hops) % n)
        if step >= first:
            above = lax.ppermute(above, axis, lowering)
    return below, above


def local(grads, slot_block):
    replicas = lax.axis_size("dp")
    slot = lax.axis_index("fsdp")
    table = lax.dynamic_index_in_dim(slot_block, lax.axis_index("dp"), 0, keepdims=False)
    chips = table.shape[0] // 2
    same_core = [[2 * p + c for p in range(chips)] for c in range(2)]
    across = [(i, i ^ 1) for i in range(2 * chips)]

    def exchanged(x):
        return lax.all_to_all(
            x, "fsdp", split_axis=0, concat_axis=0, axis_index_groups=same_core, tiled=True
        )

    first, second = assigned(table)
    core = (slot % 2)[None]
    kept = lax.dynamic_slice_in_dim(table, slot, 1, 0)
    worked = lax.dynamic_slice_in_dim(first, slot // 2, 1, 0)
    mode = jnp.where(kept >= chips, 0, jnp.where(kept == worked, 1, 2)).astype(jnp.int32)
    here = lax.axis_index("dp")[None]
    terms = ring_terms(here, grads[0], "dp")
    _, row_blocks, cols = terms[0].shape
    one, two = outgoing_pieces(here, first, second, terms, grads[0])
    one_mine = exchanged(one)
    one_mine, two = lax.optimization_barrier((one_mine, two))
    two_mine = exchanged(two)
    one_other = lax.ppermute(one_mine, "fsdp", across)
    roots, update = first_work(core, one_mine, one_other, replicas)
    update, two_mine = lax.optimization_barrier((update, two_mine))
    returned = exchanged(update)
    two_other = lax.ppermute(two_mine, "fsdp", across)
    roots = second_work(mode, core, two_mine, two_other, roots, replicas)
    result = incoming_update(first, returned, row_blocks, cols // BLK)
    return result[None], roots[None, None]


def solution(mesh):
    return jax.shard_map(
        local,
        mesh=mesh,
        in_specs=(P("dp", None, "fsdp", None, None), P()),
        out_specs=(P("dp", "fsdp", None, None), P("dp", "fsdp", None, None, None)),
        check_vma=False,
    )
```

```python
import jax
import jax.numpy as jnp
from jax import lax
from jax.experimental import pallas as pl
from jax.experimental.pallas import tpu as pltpu
from jax.sharding import PartitionSpec as P

BLK = 512
LANES = 128
PER_BLK = BLK // LANES
ITERS = 2
DAMPING = 0.1
F32 = jnp.float32
BF16 = jnp.bfloat16
VMEM_LIMIT = 24 * 1024 * 1024


def cost(flops, nbytes):
    return pl.CostEstimate(flops=flops, bytes_accessed=nbytes, transcendentals=0)


def vmem():
    return pl.BlockSpec(memory_space=pltpu.VMEM)


def smem():
    return pl.BlockSpec(memory_space=pltpu.SMEM)


def params():
    return pltpu.CompilerParams(vmem_limit_bytes=VMEM_LIMIT)


def assigned(table):
    slots = table.shape[0]
    chips = slots // 2

    def kernel(table_ref, first_ref, second_ref, spare):
        def collect(p, count):
            low, high = table_ref[2 * p], table_ref[2 * p + 1]
            two = jnp.logical_and(low < chips, high < chips)
            first_ref[p] = jnp.minimum(jnp.where(low < chips, low, high), chips)
            second_ref[p] = jnp.where(two, high, chips)
            spare[count] = high
            return count + two.astype(jnp.int32)

        def fill(p, count):
            empty = first_ref[p] == chips
            first_ref[p] = jnp.where(empty, spare[count], first_ref[p])
            return count + empty.astype(jnp.int32)

        lax.fori_loop(0, chips, collect, jnp.int32(0))
        lax.fori_loop(0, chips, fill, jnp.int32(0))

    return pl.pallas_call(
        kernel,
        out_shape=[jax.ShapeDtypeStruct((chips,), jnp.int32)] * 2,
        in_specs=[smem()],
        out_specs=[smem(), smem()],
        scratch_shapes=[pltpu.SMEM((chips + 1,), jnp.int32)],
        compiler_params=params(),
        cost_estimate=cost(0, 1024),
        name="assigned",
    )(table)


def outgoing_pieces(here, first, second, terms, parts):
    rows, row_blocks, cols = terms[0].shape
    col_blocks = cols // BLK
    group = row_blocks * col_blocks
    chips = first.shape[0]

    def kernel(
        here_ref, first_ref, second_ref, below_ref, above_ref, parts_ref, out_ref, wide, pieces
    ):
        for k in range(cols // LANES):
            at = (slice(None), slice(None), slice(k * LANES, (k + 1) * LANES))
            lanes = below_ref[at].astype(F32) + above_ref[at].astype(F32)
            lanes = lanes + parts_ref[(here_ref[0], *at)].astype(F32)
            wide[k] = lanes.reshape(rows * row_blocks, LANES)
        for rb in range(row_blocks):
            for k in range(cols // LANES):
                v, at = rb * col_blocks + k // PER_BLK, k % PER_BLK * LANES
                part = wide[k, pl.ds(rb, rows, stride=row_blocks), :]
                pieces[v, :, at : at + LANES] = part.astype(BF16)
        pieces[group] = jnp.zeros((rows, BLK), BF16)

        def place(p, carry):
            out_ref[p, 0] = pieces[first_ref[p]]
            out_ref[p, 1] = pieces[second_ref[p]]
            return carry

        lax.fori_loop(0, chips, place, 0, unroll=4)

    return pl.pallas_call(
        kernel,
        out_shape=jax.ShapeDtypeStruct((chips, 2, rows, BLK), BF16),
        in_specs=[smem(), smem(), smem(), vmem(), vmem(), vmem()],
        out_specs=vmem(),
        scratch_shapes=[
            pltpu.VMEM((cols // LANES, rows * row_blocks, LANES), F32),
            pltpu.VMEM((group + 1, rows, BLK), BF16),
        ],
        compiler_params=params(),
        cost_estimate=cost(0, 6 * chips * rows * BLK * 2),
        name="outgoing",
    )(here, first, second, *terms, parts)


def incoming_update(first, returned, row_blocks, col_blocks):
    chips, rows, _ = returned.shape
    cols = col_blocks * BLK

    def kernel(first_ref, x_ref, out_ref, wide, pieces):
        def place(s, carry):
            pieces[first_ref[s]] = x_ref[s]
            return carry

        lax.fori_loop(0, chips, place, 0, unroll=4)
        for rb in range(row_blocks):
            for k in range(cols // LANES):
                v, at = rb * col_blocks + k // PER_BLK, k % PER_BLK * LANES
                part = pieces[v, :, at : at + LANES].astype(F32)
                wide[k, pl.ds(rb, rows, stride=row_blocks), :] = part
        for k in range(cols // LANES):
            lanes = wide[k].reshape(rows, row_blocks, LANES)
            out_ref[:, :, k * LANES : (k + 1) * LANES] = lanes.astype(BF16)

    return pl.pallas_call(
        kernel,
        out_shape=jax.ShapeDtypeStruct((rows, row_blocks, cols), BF16),
        in_specs=[smem(), vmem()],
        out_specs=vmem(),
        scratch_shapes=[
            pltpu.VMEM((cols // LANES, rows * row_blocks, LANES), F32),
            pltpu.VMEM((chips, rows, BLK), BF16),
        ],
        compiler_params=params(),
        cost_estimate=cost(0, 3 * chips * rows * BLK * 2),
        name="incoming",
    )(first, returned)


def dot(a, b, contract=((1,), (0,))):
    return lax.dot_general(a, b, (contract, ((), ())), preferred_element_type=F32)


def newton_root(stat, total, eye):
    damped = stat + (DAMPING * total / BLK + 1e-06) * eye
    scale = jnp.sqrt(jnp.sum(damped * damped)) / 4.0
    matrix = damped * (1.0 / scale)
    root = None
    for iteration in range(ITERS):
        factor = 1.25 * eye - 0.25 * matrix
        factor_low = factor.astype(BF16)
        if iteration == 0:
            root = (lax.rsqrt(jnp.sqrt(scale)) * factor).astype(BF16)
        else:
            root = dot(root, factor_low).astype(BF16)
        if iteration + 1 < ITERS:
            square = dot(factor_low, factor_low).astype(BF16)
            fourth = dot(square, square).astype(BF16)
            matrix = dot(fourth, matrix.astype(BF16))
    return root


def whole_block(core_ref, mine_ref, other_ref, which, halves):
    halves[:, core_ref[0]] = mine_ref[:, which].astype(F32)
    halves[:, 1 - core_ref[0]] = other_ref[:, which].astype(F32)
    return halves[...].reshape(BLK, BLK)


def both_roots(wide, replicas):
    eye = (
        lax.broadcasted_iota(jnp.int32, (BLK, BLK), 0)
        == lax.broadcasted_iota(jnp.int32, (BLK, BLK), 1)
    ).astype(F32)
    x = wide.astype(BF16)
    scale = 1.0 / (replicas * replicas)
    total = jnp.sum(wide * wide) * scale
    left = newton_root(dot(x, x, ((1,), (1,))) * scale, total, eye)
    right = newton_root(dot(x, x, ((0,), (0,))) * scale, total, eye)
    return x, total, left, right


def first_work(core, mine, other, replicas):
    chips, _, rows, _ = mine.shape

    def kernel(core_ref, mine_ref, other_ref, roots_ref, update_ref, halves):
        wide = whole_block(core_ref, mine_ref, other_ref, 0, halves)
        x, total, left, right = both_roots(wide, replicas)
        roots_ref[0] = left
        roots_ref[1] = right
        partial = (dot(left, x) * (1.0 / replicas)).astype(BF16)
        direction = dot(partial, right)
        count = BLK * BLK
        grad_rms = jnp.sqrt(total / count)
        dir_rms = jnp.sqrt(jnp.sum(direction * direction) / count + 1e-06)
        halves[...] = (-(grad_rms / dir_rms) * direction).reshape(chips, 2, rows, BLK)
        update_ref[...] = halves[:, core_ref[0]].astype(BF16)

    return pl.pallas_call(
        kernel,
        out_shape=(
            jax.ShapeDtypeStruct((2, BLK, BLK), BF16),
            jax.ShapeDtypeStruct((chips, rows, BLK), BF16),
        ),
        in_specs=[smem(), vmem(), vmem()],
        out_specs=(vmem(), vmem()),
        scratch_shapes=[pltpu.VMEM((chips, 2, rows, BLK), F32)],
        compiler_params=params(),
        cost_estimate=cost(24 * BLK**3, 8 * BLK * BLK),
        name="first_work",
    )(core, mine, other)


def second_work(mode, core, mine, other, roots, replicas):
    chips, _, rows, _ = mine.shape

    def kernel(mode_ref, core_ref, mine_ref, other_ref, roots_ref, out_ref, halves):
        @pl.when(mode_ref[0] == 0)
        def _():
            out_ref[...] = jnp.zeros_like(out_ref)

        @pl.when(mode_ref[0] == 1)
        def _():
            out_ref[...] = roots_ref[...]

        @pl.when(mode_ref[0] == 2)
        def _():
            wide = whole_block(core_ref, mine_ref, other_ref, 1, halves)
            _, _, left, right = both_roots(wide, replicas)
            out_ref[0] = left
            out_ref[1] = right

    return pl.pallas_call(
        kernel,
        out_shape=jax.ShapeDtypeStruct((2, BLK, BLK), BF16),
        in_specs=[smem(), smem(), vmem(), vmem(), vmem()],
        out_specs=vmem(),
        scratch_shapes=[pltpu.VMEM((chips, 2, rows, BLK), F32)],
        compiler_params=params(),
        cost_estimate=cost(20 * BLK**3, 8 * BLK * BLK),
        name="second_work",
    )(mode, core, mine, other, roots)


def part_at(parts_ref, here_ref, offset):
    return parts_ref[lax.rem(here_ref[0] + offset, parts_ref.shape[0])]


def picked(here, parts, offsets):
    def kernel(here_ref, parts_ref, *out_refs):
        for offset, out_ref in zip(offsets, out_refs):
            out_ref[...] = part_at(parts_ref, here_ref, offset)

    return pl.pallas_call(
        kernel,
        out_shape=[jax.ShapeDtypeStruct(parts.shape[1:], BF16)] * len(offsets),
        in_specs=[smem(), vmem()],
        out_specs=[vmem()] * len(offsets),
        compiler_params=params(),
        cost_estimate=cost(0, 4 * parts[0].size * len(offsets)),
        name="picked",
    )(here, parts)


def added(here, total, parts, offset):
    def kernel(here_ref, total_ref, parts_ref, out_ref):
        own = part_at(parts_ref, here_ref, offset).astype(F32)
        out_ref[...] = (total_ref[...].astype(F32) + own).astype(BF16)

    return pl.pallas_call(
        kernel,
        out_shape=jax.ShapeDtypeStruct(total.shape, BF16),
        in_specs=[smem(), vmem(), vmem()],
        out_specs=vmem(),
        compiler_params=params(),
        cost_estimate=cost(total.size, 6 * total.size),
        name="added",
    )(here, total, parts)


def ring_terms(here, parts, axis):
    n = parts.shape[0]
    raising = [(i, (i + 1) % n) for i in range(n)]
    lowering = [(i, (i - 1) % n) for i in range(n)]
    hops = n // 2
    first = 2 * hops + 1 - n
    below, above = picked(here, parts, (hops, (first - hops) % n))
    for step in range(hops):
        if step > 0:
            below = added(here, below, parts, hops - step)
        below = lax.ppermute(below, axis, raising)
        if step > first:
            above = added(here, above, parts, (step - hops) % n)
        if step >= first:
            above = lax.ppermute(above, axis, lowering)
    return below, above


def local(grads, slot_block):
    replicas = lax.axis_size("dp")
    slot = lax.axis_index("fsdp")
    table = lax.dynamic_index_in_dim(slot_block, lax.axis_index("dp"), 0, keepdims=False)
    chips = table.shape[0] // 2
    same_core = [[2 * p + c for p in range(chips)] for c in range(2)]
    across = [(i, i ^ 1) for i in range(2 * chips)]

    def exchanged(x):
        return lax.all_to_all(
            x, "fsdp", split_axis=0, concat_axis=0, axis_index_groups=same_core, tiled=True
        )

    first, second = assigned(table)
    core = (slot % 2)[None]
    kept = lax.dynamic_slice_in_dim(table, slot, 1, 0)
    worked = lax.dynamic_slice_in_dim(first, slot // 2, 1, 0)
    mode = jnp.where(kept >= chips, 0, jnp.where(kept == worked, 1, 2)).astype(jnp.int32)
    here = lax.axis_index("dp")[None]
    terms = ring_terms(here, grads[0], "dp")
    _, row_blocks, cols = terms[0].shape
    mine = exchanged(outgoing_pieces(here, first, second, terms, grads[0]))
    other = lax.ppermute(mine, "fsdp", across)
    roots, update = first_work(core, mine, other, replicas)
    returned = exchanged(update)
    roots = second_work(mode, core, mine, other, roots, replicas)
    result = incoming_update(first, returned, row_blocks, cols // BLK)
    return result[None], roots[None, None]


def solution(mesh):
    return jax.shard_map(
        local,
        mesh=mesh,
        in_specs=(P("dp", None, "fsdp", None, None), P()),
        out_specs=(P("dp", "fsdp", None, None), P("dp", "fsdp", None, None, None)),
        check_vma=False,
    )
```

```python
import jax
import jax.numpy as jnp
from jax import lax
from jax.experimental import pallas as pl
from jax.experimental.pallas import tpu as pltpu
from jax.sharding import PartitionSpec as P

BLK = 512
LANES = 128
PER_BLK = BLK // LANES
STRIP = 64
ITERS = 2
DAMPING = 0.1
F32 = jnp.float32
BF16 = jnp.bfloat16
VMEM_LIMIT = 24 * 1024 * 1024
PICK_LIMIT = 61 * 1024 * 1024
STAGE_LIMIT = 50 * 1024 * 1024


def cost(flops, nbytes):
    return pl.CostEstimate(flops=flops, bytes_accessed=nbytes, transcendentals=0)


def vmem():
    return pl.BlockSpec(memory_space=pltpu.VMEM)


def smem():
    return pl.BlockSpec(memory_space=pltpu.SMEM)


def params(limit=VMEM_LIMIT):
    return pltpu.CompilerParams(vmem_limit_bytes=limit)


def assigned(here, slot, slot_block):
    chips = slot_block.shape[1] // 2

    def kernel(here_ref, slot_ref, table_ref, first_ref, second_ref, mode_ref, spare):
        row = here_ref[0]

        def collect(p, count):
            low, high = table_ref[row, 2 * p], table_ref[row, 2 * p + 1]
            two = jnp.logical_and(low < chips, high < chips)
            first_ref[p] = jnp.minimum(jnp.where(low < chips, low, high), chips)
            second_ref[p] = jnp.where(two, high, chips)
            spare[count] = high
            return count + two.astype(jnp.int32)

        def fill(p, count):
            empty = first_ref[p] == chips
            first_ref[p] = jnp.where(empty, spare[count], first_ref[p])
            return count + empty.astype(jnp.int32)

        lax.fori_loop(0, chips, collect, jnp.int32(0))
        lax.fori_loop(0, chips, fill, jnp.int32(0))
        kept = table_ref[row, slot_ref[0]]
        same = kept == first_ref[lax.div(slot_ref[0], 2)]
        mode_ref[0] = jnp.where(kept < chips, jnp.where(same, 1, 2), 0)

    return pl.pallas_call(
        kernel,
        out_shape=[jax.ShapeDtypeStruct((n,), jnp.int32) for n in (chips, chips, 1)],
        in_specs=[smem(), smem(), smem()],
        out_specs=[smem(), smem(), smem()],
        scratch_shapes=[pltpu.SMEM((chips + 1,), jnp.int32)],
        compiler_params=params(),
        cost_estimate=cost(0, 1024),
        name="assigned",
    )(here, slot, slot_block)


def outgoing_pieces(first, second, terms):
    rows, row_blocks, cols = terms[0].shape
    col_blocks = cols // BLK
    group = row_blocks * col_blocks
    chips = first.shape[0]

    def kernel(
        first_ref, second_ref, below_ref, above_ref, own_ref, out_ref, wide, pieces
    ):
        for k in range(cols // LANES):
            at = (slice(None), slice(None), slice(k * LANES, (k + 1) * LANES))
            lanes = below_ref[at].astype(F32) + above_ref[at].astype(F32)
            lanes = lanes + own_ref[at].astype(F32)
            wide[k] = lanes.reshape(rows * row_blocks, LANES)
        for rb in range(row_blocks):
            for k in range(cols // LANES):
                v, at = rb * col_blocks + k // PER_BLK, k % PER_BLK * LANES
                part = wide[k, pl.ds(rb, rows, stride=row_blocks), :]
                pieces[v, :, at : at + LANES] = part.astype(BF16)
        pieces[group] = jnp.zeros((rows, BLK), BF16)

        def place(p, carry):
            out_ref[p, 0] = pieces[first_ref[p]]
            out_ref[p, 1] = pieces[second_ref[p]]
            return carry

        lax.fori_loop(0, chips, place, 0, unroll=4)

    return pl.pallas_call(
        kernel,
        out_shape=jax.ShapeDtypeStruct((chips, 2, rows, BLK), BF16),
        in_specs=[smem(), smem(), vmem(), vmem(), vmem()],
        out_specs=vmem(),
        scratch_shapes=[
            pltpu.VMEM((cols // LANES, rows * row_blocks, LANES), F32),
            pltpu.VMEM((group + 1, rows, BLK), BF16),
        ],
        compiler_params=params(),
        cost_estimate=cost(0, 6 * chips * rows * BLK * 2),
        name="outgoing",
    )(first, second, *terms)


def incoming_update(first, returned, row_blocks, col_blocks):
    chips, rows, _ = returned.shape
    cols = col_blocks * BLK

    def kernel(first_ref, x_ref, out_ref, wide, pieces):
        def place(s, carry):
            pieces[first_ref[s]] = x_ref[s]
            return carry

        lax.fori_loop(0, chips, place, 0, unroll=4)
        for rb in range(row_blocks):
            for k in range(cols // LANES):
                v, at = rb * col_blocks + k // PER_BLK, k % PER_BLK * LANES
                part = pieces[v, :, at : at + LANES].astype(F32)
                wide[k, pl.ds(rb, rows, stride=row_blocks), :] = part
        for k in range(cols // LANES):
            lanes = wide[k].reshape(rows, row_blocks, LANES)
            out_ref[:, :, k * LANES : (k + 1) * LANES] = lanes.astype(BF16)

    return pl.pallas_call(
        kernel,
        out_shape=jax.ShapeDtypeStruct((rows, row_blocks, cols), BF16),
        in_specs=[smem(), vmem()],
        out_specs=vmem(),
        scratch_shapes=[
            pltpu.VMEM((cols // LANES, rows * row_blocks, LANES), F32),
            pltpu.VMEM((chips, rows, BLK), BF16),
        ],
        compiler_params=params(),
        cost_estimate=cost(0, 3 * chips * rows * BLK * 2),
        name="incoming",
    )(first, returned)


def dot(a, b, contract=((1,), (0,))):
    return lax.dot_general(a, b, (contract, ((), ())), preferred_element_type=F32)


def strips(rows=BLK):
    return [slice(at, at + STRIP) for at in range(0, rows, STRIP)]


def folded(x):
    return jnp.sum(x.reshape(-1, 8, x.shape[-1]), axis=0)


def put_linear(out_ref, in_ref, times, diagonal):
    row = lax.broadcasted_iota(jnp.int32, (STRIP, LANES), 0)
    lane = lax.broadcasted_iota(jnp.int32, (STRIP, LANES), 1)
    for at in strips():
        x = in_ref[at, :] * times
        out_ref[at, :] = x.astype(BF16)
        left = at.start // LANES * LANES
        lanes = slice(left, left + LANES)
        eye = jnp.where(row + (at.start - left) == lane, diagonal, 0.0)
        out_ref[at, lanes] = (x[:, lanes] + eye).astype(BF16)


def newton_root(gram, total, scale, low, rest, root):
    shift = DAMPING * total / BLK + 1e-06
    squares = sum(folded(gram[at, :] * gram[at, :]) for at in strips())
    squares = jnp.sum(squares) * (scale * scale)
    norm = jnp.sqrt(squares + 2.0 * shift * total + BLK * shift * shift) / 4.0
    times, diagonal = scale / norm, shift / norm
    start = lax.rsqrt(jnp.sqrt(norm))
    for iteration in range(ITERS):
        put_linear(low, gram, -0.25 * times, 1.25 - 0.25 * diagonal)
        if iteration == 0:
            put_linear(root, gram, -0.25 * times * start, (1.25 - 0.25 * diagonal) * start)
        else:
            root[...] = dot(root[...], low[...]).astype(BF16)
        if iteration + 1 < ITERS:
            put_linear(rest, gram, times, diagonal)
            square = dot(low[...], low[...]).astype(BF16)
            fourth = dot(square, square).astype(BF16)
            gram[...] = dot(fourth, rest[...])
            times, diagonal = 1.0, 0.0


def whole_block(core_ref, mine_ref, other_ref, which, halves, block):
    halves[:, core_ref[0]] = mine_ref[:, which].astype(F32)
    halves[:, 1 - core_ref[0]] = other_ref[:, which].astype(F32)
    chips, _, rows, _ = halves.shape
    per_strip = STRIP // (2 * rows)
    squares = 0.0
    for k, at in enumerate(strips()):
        x = halves[k * per_strip : (k + 1) * per_strip].reshape(STRIP, BLK)
        block[at, :] = x.astype(BF16)
        squares += folded(x * x)
    return jnp.sum(squares)


def buffers(chips, rows):
    return [
        pltpu.VMEM((chips, 2, rows, BLK), F32),
        pltpu.VMEM((BLK, BLK), F32),
        pltpu.VMEM((BLK, BLK), BF16),
        pltpu.VMEM((BLK, BLK), BF16),
        pltpu.VMEM((BLK, BLK), BF16),
    ]


def first_work(core, mine, other, replicas):
    chips, _, rows, _ = mine.shape
    scale = 1.0 / (replicas * replicas)

    def kernel(core_ref, mine_ref, other_ref, right, update_ref, halves, gram, block, low, rest):
        total = whole_block(core_ref, mine_ref, other_ref, 0, halves, block) * scale
        gram[...] = dot(block[...], block[...], ((0,), (0,)))
        newton_root(gram, total, scale, low, rest, right)
        low[...] = (dot(block[...], right[...]) * (1.0 / replicas)).astype(BF16)
        halves[...] = dot(low[...], right[...]).reshape(halves.shape)
        squares = sum(folded(halves[p] * halves[p]) for p in range(chips))
        count = BLK * BLK
        grad_rms = jnp.sqrt(total / count)
        dir_rms = jnp.sqrt(jnp.sum(squares) / count + 1e-06)
        factor = -(grad_rms / dir_rms)
        for p in range(0, chips, 4):
            update_ref[p : p + 4] = (halves[p : p + 4, core_ref[0]] * factor).astype(BF16)

    return pl.pallas_call(
        kernel,
        out_shape=(
            jax.ShapeDtypeStruct((BLK, BLK), BF16),
            jax.ShapeDtypeStruct((chips, rows, BLK), BF16),
        ),
        in_specs=[smem(), vmem(), vmem()],
        out_specs=(vmem(), vmem()),
        scratch_shapes=buffers(chips, rows),
        compiler_params=params(),
        cost_estimate=cost(14 * BLK**3, 8 * BLK * BLK),
        name="first_work",
    )(core, mine, other)


def slot_work(mode, core, mine, other, first_right, replicas):
    chips, _, rows, _ = mine.shape
    scale = 1.0 / (replicas * replicas)

    def kernel(mode_ref, core_ref, mine_ref, other_ref, right_ref, out_ref, halves, gram, block, low, rest):
        def left_root(which):
            total = whole_block(core_ref, mine_ref, other_ref, which, halves, block) * scale
            gram[...] = dot(block[...], block[...], ((1,), (1,)))
            newton_root(gram, total, scale, low, rest, out_ref.at[0])
            return total

        @pl.when(mode_ref[0] == 0)
        def _():
            out_ref[...] = jnp.zeros_like(out_ref)

        @pl.when(mode_ref[0] == 1)
        def _():
            left_root(0)
            out_ref[1] = right_ref[...]

        @pl.when(mode_ref[0] == 2)
        def _():
            total = left_root(1)
            gram[...] = dot(block[...], block[...], ((0,), (0,)))
            newton_root(gram, total, scale, low, rest, out_ref.at[1])

    return pl.pallas_call(
        kernel,
        out_shape=jax.ShapeDtypeStruct((2, BLK, BLK), BF16),
        in_specs=[smem(), smem(), vmem(), vmem(), vmem()],
        out_specs=vmem(),
        scratch_shapes=buffers(chips, rows),
        compiler_params=params(),
        cost_estimate=cost(20 * BLK**3, 8 * BLK * BLK),
        name="slot_work",
    )(mode, core, mine, other, first_right)


def part_of(parts_ref, here_ref, offset):
    return parts_ref.at[lax.rem(here_ref[0] + offset, parts_ref.shape[0])]


def picked(here, parts, offsets):
    def kernel(here_ref, parts_ref, *refs):
        outs, sems = refs[: len(offsets)], refs[len(offsets)]
        copies = [
            pltpu.make_async_copy(part_of(parts_ref, here_ref, offset), out, sems.at[k])
            for k, (offset, out) in enumerate(zip(offsets, outs))
        ]
        for copy in copies:
            copy.start()
        for copy in copies:
            copy.wait()

    return pl.pallas_call(
        kernel,
        out_shape=[jax.ShapeDtypeStruct(parts.shape[1:], BF16)] * len(offsets),
        in_specs=[smem(), pl.BlockSpec(memory_space=pltpu.HBM)],
        out_specs=[vmem()] * len(offsets),
        scratch_shapes=[pltpu.SemaphoreType.DMA((len(offsets),))],
        compiler_params=params(PICK_LIMIT),
        cost_estimate=cost(0, 4 * parts[0].size * len(offsets)),
        name="picked",
    )(here, parts)


def staged(parts):
    def kernel(parts_ref, out_ref, sem):
        copy = pltpu.make_async_copy(parts_ref, out_ref, sem.at[0])
        copy.start()
        copy.wait()

    return pl.pallas_call(
        kernel,
        out_shape=jax.ShapeDtypeStruct(parts.shape, BF16),
        in_specs=[pl.BlockSpec(memory_space=pltpu.HBM)],
        out_specs=vmem(),
        scratch_shapes=[pltpu.SemaphoreType.DMA((1,))],
        compiler_params=params(STAGE_LIMIT),
        cost_estimate=cost(0, 4 * parts.size),
        name="staged",
    )(parts)


def added(here, total, parts, offset):
    def kernel(here_ref, total_ref, parts_ref, out_ref):
        own = part_of(parts_ref, here_ref, offset)[...].astype(F32)
        out_ref[...] = (total_ref[...].astype(F32) + own).astype(BF16)

    return pl.pallas_call(
        kernel,
        out_shape=jax.ShapeDtypeStruct(total.shape, BF16),
        in_specs=[smem(), vmem(), vmem()],
        out_specs=vmem(),
        compiler_params=params(),
        cost_estimate=cost(total.size, 6 * total.size),
        name="added",
    )(here, total, parts)


def ring_terms(here, parts, axis):
    n = parts.shape[0]
    raising = [(i, (i + 1) % n) for i in range(n)]
    lowering = [(i, (i - 1) % n) for i in range(n)]
    hops = n // 2
    first = 2 * hops + 1 - n
    below, above, own = picked(here, parts, (hops, (first - hops) % n, 0))
    below, parts = lax.optimization_barrier((below, parts))
    parts = staged(parts)
    for step in range(hops):
        if step > 0:
            below = added(here, below, parts, hops - step)
        below = lax.ppermute(below, axis, raising)
        if step > first:
            above = added(here, above, parts, (step - hops) % n)
        if step >= first:
            above = lax.ppermute(above, axis, lowering)
    return below, above, own


def local(grads, slot_block):
    replicas = lax.axis_size("dp")
    here, slot = lax.axis_index("dp")[None], lax.axis_index("fsdp")[None]
    core = slot % 2
    chips = slot_block.shape[1] // 2
    same_core = [[2 * p + c for p in range(chips)] for c in range(2)]
    across = [(i, i ^ 1) for i in range(2 * chips)]

    def exchanged(x):
        return lax.all_to_all(
            x, "fsdp", split_axis=0, concat_axis=0, axis_index_groups=same_core, tiled=True
        )

    first, second, mode = assigned(here, slot, slot_block)
    terms = ring_terms(here, grads[0], "dp")
    _, row_blocks, cols = terms[0].shape
    mine = exchanged(outgoing_pieces(first, second, terms))
    other = lax.ppermute(mine, "fsdp", across)
    right, update = first_work(core, mine, other, replicas)
    returned = exchanged(update)
    roots = slot_work(mode, core, mine, other, right, replicas)
    result = incoming_update(first, returned, row_blocks, cols // BLK)
    return result[None], roots[None, None]


def solution(mesh):
    return jax.shard_map(
        local,
        mesh=mesh,
        in_specs=(P("dp", None, "fsdp", None, None), P()),
        out_specs=(P("dp", "fsdp", None, None), P("dp", "fsdp", None, None, None)),
        check_vma=False,
    )
```

```python
import jax
import jax.numpy as jnp
from jax import lax
from jax.experimental import pallas as pl
from jax.experimental.pallas import tpu as pltpu
from jax.sharding import PartitionSpec as P

BLK = 512
LANES = 128
PER_BLK = BLK // LANES
STRIP = 64
ITERS = 2
DAMPING = 0.1
F32 = jnp.float32
BF16 = jnp.bfloat16
VMEM_LIMIT = 24 * 1024 * 1024
PICK_LIMIT = 61 * 1024 * 1024
STAGE_LIMIT = 50 * 1024 * 1024


def cost(flops, nbytes):
    return pl.CostEstimate(flops=flops, bytes_accessed=nbytes, transcendentals=0)


def vmem():
    return pl.BlockSpec(memory_space=pltpu.VMEM)


def smem():
    return pl.BlockSpec(memory_space=pltpu.SMEM)


def params(limit=VMEM_LIMIT):
    return pltpu.CompilerParams(vmem_limit_bytes=limit)


def assigned(here, slot, slot_block):
    chips = slot_block.shape[1] // 2

    def kernel(here_ref, slot_ref, table_ref, first_ref, second_ref, mode_ref, spare):
        row = here_ref[0]

        def collect(p, count):
            low, high = table_ref[row, 2 * p], table_ref[row, 2 * p + 1]
            two = jnp.logical_and(low < chips, high < chips)
            first_ref[p] = jnp.minimum(jnp.where(low < chips, low, high), chips)
            second_ref[p] = jnp.where(two, high, chips)
            spare[count] = high
            return count + two.astype(jnp.int32)

        def fill(p, count):
            empty = first_ref[p] == chips
            first_ref[p] = jnp.where(empty, spare[count], first_ref[p])
            return count + empty.astype(jnp.int32)

        lax.fori_loop(0, chips, collect, jnp.int32(0))
        lax.fori_loop(0, chips, fill, jnp.int32(0))
        kept = table_ref[row, slot_ref[0]]
        same = kept == first_ref[lax.div(slot_ref[0], 2)]
        mode_ref[0] = jnp.where(kept < chips, jnp.where(same, 1, 2), 0)

    return pl.pallas_call(
        kernel,
        out_shape=[jax.ShapeDtypeStruct((n,), jnp.int32) for n in (chips, chips, 1)],
        in_specs=[smem(), smem(), smem()],
        out_specs=[smem(), smem(), smem()],
        scratch_shapes=[pltpu.SMEM((chips + 1,), jnp.int32)],
        compiler_params=params(),
        cost_estimate=cost(0, 1024),
        name="assigned",
    )(here, slot, slot_block)


def outgoing_pieces(first, second, terms):
    rows, row_blocks, cols = terms[0].shape
    col_blocks = cols // BLK
    group = row_blocks * col_blocks
    chips = first.shape[0]

    def kernel(
        first_ref, second_ref, below_ref, above_ref, own_ref, out_ref, wide, pieces
    ):
        for k in range(cols // LANES):
            at = (slice(None), slice(None), slice(k * LANES, (k + 1) * LANES))
            lanes = below_ref[at].astype(F32) + above_ref[at].astype(F32)
            lanes = lanes + own_ref[at].astype(F32)
            wide[k] = lanes.reshape(rows * row_blocks, LANES)
        for rb in range(row_blocks):
            for k in range(cols // LANES):
                v, at = rb * col_blocks + k // PER_BLK, k % PER_BLK * LANES
                part = wide[k, pl.ds(rb, rows, stride=row_blocks), :]
                pieces[v, :, at : at + LANES] = part.astype(BF16)
        pieces[group] = jnp.zeros((rows, BLK), BF16)

        def place(p, carry):
            out_ref[p, 0] = pieces[first_ref[p]]
            out_ref[p, 1] = pieces[second_ref[p]]
            return carry

        lax.fori_loop(0, chips, place, 0, unroll=4)

    return pl.pallas_call(
        kernel,
        out_shape=jax.ShapeDtypeStruct((chips, 2, rows, BLK), BF16),
        in_specs=[smem(), smem(), vmem(), vmem(), vmem()],
        out_specs=vmem(),
        scratch_shapes=[
            pltpu.VMEM((cols // LANES, rows * row_blocks, LANES), F32),
            pltpu.VMEM((group + 1, rows, BLK), BF16),
        ],
        compiler_params=params(),
        cost_estimate=cost(0, 6 * chips * rows * BLK * 2),
        name="outgoing",
    )(first, second, *terms)


def incoming_update(first, returned, row_blocks, col_blocks):
    chips, rows, _ = returned.shape
    cols = col_blocks * BLK

    def kernel(first_ref, x_ref, out_ref, wide, pieces):
        def place(s, carry):
            pieces[first_ref[s]] = x_ref[s]
            return carry

        lax.fori_loop(0, chips, place, 0, unroll=4)
        for rb in range(row_blocks):
            for k in range(cols // LANES):
                v, at = rb * col_blocks + k // PER_BLK, k % PER_BLK * LANES
                part = pieces[v, :, at : at + LANES].astype(F32)
                wide[k, pl.ds(rb, rows, stride=row_blocks), :] = part
        for k in range(cols // LANES):
            lanes = wide[k].reshape(rows, row_blocks, LANES)
            out_ref[:, :, k * LANES : (k + 1) * LANES] = lanes.astype(BF16)

    return pl.pallas_call(
        kernel,
        out_shape=jax.ShapeDtypeStruct((rows, row_blocks, cols), BF16),
        in_specs=[smem(), vmem()],
        out_specs=vmem(),
        scratch_shapes=[
            pltpu.VMEM((cols // LANES, rows * row_blocks, LANES), F32),
            pltpu.VMEM((chips, rows, BLK), BF16),
        ],
        compiler_params=params(),
        cost_estimate=cost(0, 3 * chips * rows * BLK * 2),
        name="incoming",
    )(first, returned)


def dot(a, b, contract=((1,), (0,))):
    return lax.dot_general(a, b, (contract, ((), ())), preferred_element_type=F32)


def strips(rows=BLK):
    return [slice(at, at + STRIP) for at in range(0, rows, STRIP)]


def folded(x):
    return jnp.sum(x.reshape(-1, 8, x.shape[-1]), axis=0)


def put_linear(out_ref, in_ref, times, diagonal):
    row = lax.broadcasted_iota(jnp.int32, (STRIP, LANES), 0)
    lane = lax.broadcasted_iota(jnp.int32, (STRIP, LANES), 1)
    for at in strips():
        x = in_ref[at, :] * times
        out_ref[at, :] = x.astype(BF16)
        left = at.start // LANES * LANES
        lanes = slice(left, left + LANES)
        eye = jnp.where(row + (at.start - left) == lane, diagonal, 0.0)
        out_ref[at, lanes] = (x[:, lanes] + eye).astype(BF16)


def newton_root(gram, total, scale, low, rest, root):
    shift = DAMPING * total / BLK + 1e-06
    squares = sum(folded(gram[at, :] * gram[at, :]) for at in strips())
    squares = jnp.sum(squares) * (scale * scale)
    norm = jnp.sqrt(squares + 2.0 * shift * total + BLK * shift * shift) / 4.0
    times, diagonal = scale / norm, shift / norm
    start = lax.rsqrt(jnp.sqrt(norm))
    for iteration in range(ITERS):
        put_linear(low, gram, -0.25 * times, 1.25 - 0.25 * diagonal)
        if iteration == 0:
            put_linear(root, gram, -0.25 * times * start, (1.25 - 0.25 * diagonal) * start)
        else:
            root[...] = dot(root[...], low[...]).astype(BF16)
        if iteration + 1 < ITERS:
            put_linear(rest, gram, times, diagonal)
            square = dot(low[...], low[...]).astype(BF16)
            fourth = dot(square, square).astype(BF16)
            gram[...] = dot(fourth, rest[...])
            times, diagonal = 1.0, 0.0


def whole_block(core_ref, mine_ref, other_ref, which, halves, block):
    halves[:, core_ref[0]] = mine_ref[:, which].astype(F32)
    halves[:, 1 - core_ref[0]] = other_ref[:, which].astype(F32)
    chips, _, rows, _ = halves.shape
    per_strip = STRIP // (2 * rows)
    squares = 0.0
    for k, at in enumerate(strips()):
        x = halves[k * per_strip : (k + 1) * per_strip].reshape(STRIP, BLK)
        block[at, :] = x.astype(BF16)
        squares += folded(x * x)
    return jnp.sum(squares)


def buffers(chips, rows):
    return [
        pltpu.VMEM((chips, 2, rows, BLK), F32),
        pltpu.VMEM((BLK, BLK), F32),
        pltpu.VMEM((BLK, BLK), BF16),
        pltpu.VMEM((BLK, BLK), BF16),
        pltpu.VMEM((BLK, BLK), BF16),
    ]


def first_work(core, mine, other, replicas):
    chips, _, rows, _ = mine.shape
    scale = 1.0 / (replicas * replicas)

    def kernel(core_ref, mine_ref, other_ref, right, update_ref, halves, gram, block, low, rest):
        total = whole_block(core_ref, mine_ref, other_ref, 0, halves, block) * scale
        gram[...] = dot(block[...], block[...], ((0,), (0,)))
        newton_root(gram, total, scale, low, rest, right)
        low[...] = (dot(block[...], right[...]) * (1.0 / replicas)).astype(BF16)
        halves[...] = dot(low[...], right[...]).reshape(halves.shape)
        squares = sum(folded(halves[p] * halves[p]) for p in range(chips))
        count = BLK * BLK
        grad_rms = jnp.sqrt(total / count)
        dir_rms = jnp.sqrt(jnp.sum(squares) / count + 1e-06)
        factor = -(grad_rms / dir_rms)
        for p in range(0, chips, 4):
            update_ref[p : p + 4] = (halves[p : p + 4, core_ref[0]] * factor).astype(BF16)

    return pl.pallas_call(
        kernel,
        out_shape=(
            jax.ShapeDtypeStruct((BLK, BLK), BF16),
            jax.ShapeDtypeStruct((chips, rows, BLK), BF16),
        ),
        in_specs=[smem(), vmem(), vmem()],
        out_specs=(vmem(), vmem()),
        scratch_shapes=buffers(chips, rows),
        compiler_params=params(),
        cost_estimate=cost(14 * BLK**3, 8 * BLK * BLK),
        name="first_work",
    )(core, mine, other)


def slot_work(mode, core, mine, other, first_right, replicas):
    chips, _, rows, _ = mine.shape
    scale = 1.0 / (replicas * replicas)

    def kernel(mode_ref, core_ref, mine_ref, other_ref, right_ref, out_ref, halves, gram, block, low, rest):
        def left_root(which):
            total = whole_block(core_ref, mine_ref, other_ref, which, halves, block) * scale
            gram[...] = dot(block[...], block[...], ((1,), (1,)))
            newton_root(gram, total, scale, low, rest, out_ref.at[0])
            return total

        @pl.when(mode_ref[0] == 0)
        def _():
            out_ref[...] = jnp.zeros_like(out_ref)

        @pl.when(mode_ref[0] == 1)
        def _():
            left_root(0)
            out_ref[1] = right_ref[...]

        @pl.when(mode_ref[0] == 2)
        def _():
            total = left_root(1)
            gram[...] = dot(block[...], block[...], ((0,), (0,)))
            newton_root(gram, total, scale, low, rest, out_ref.at[1])

    return pl.pallas_call(
        kernel,
        out_shape=jax.ShapeDtypeStruct((2, BLK, BLK), BF16),
        in_specs=[smem(), smem(), vmem(), vmem(), vmem()],
        out_specs=vmem(),
        scratch_shapes=buffers(chips, rows),
        compiler_params=params(),
        cost_estimate=cost(20 * BLK**3, 8 * BLK * BLK),
        name="slot_work",
    )(mode, core, mine, other, first_right)


def part_of(parts_ref, here_ref, offset):
    return parts_ref.at[lax.rem(here_ref[0] + offset, parts_ref.shape[0])]


def picked(here, parts, offset):
    def kernel(here_ref, parts_ref, out_ref, sem):
        copy = pltpu.make_async_copy(part_of(parts_ref, here_ref, offset), out_ref, sem.at[0])
        copy.start()
        copy.wait()

    return pl.pallas_call(
        kernel,
        out_shape=jax.ShapeDtypeStruct(parts.shape[1:], BF16),
        in_specs=[smem(), pl.BlockSpec(memory_space=pltpu.HBM)],
        out_specs=vmem(),
        scratch_shapes=[pltpu.SemaphoreType.DMA((1,))],
        compiler_params=params(PICK_LIMIT),
        cost_estimate=cost(0, 4 * parts[0].size),
        name="picked",
    )(here, parts)


def staged(here, parts):
    def kernel(here_ref, parts_ref, all_ref, own_ref, sems):
        copies = [
            pltpu.make_async_copy(parts_ref, all_ref, sems.at[0]),
            pltpu.make_async_copy(part_of(parts_ref, here_ref, 0), own_ref, sems.at[1]),
        ]
        for copy in copies:
            copy.start()
        for copy in copies:
            copy.wait()

    return pl.pallas_call(
        kernel,
        out_shape=[
            jax.ShapeDtypeStruct(parts.shape, BF16),
            jax.ShapeDtypeStruct(parts.shape[1:], BF16),
        ],
        in_specs=[smem(), pl.BlockSpec(memory_space=pltpu.HBM)],
        out_specs=[vmem(), vmem()],
        scratch_shapes=[pltpu.SemaphoreType.DMA((2,))],
        compiler_params=params(STAGE_LIMIT),
        cost_estimate=cost(0, 4 * parts.size),
        name="staged",
    )(here, parts)


def added(here, total, parts, offset):
    def kernel(here_ref, total_ref, parts_ref, out_ref):
        own = part_of(parts_ref, here_ref, offset)[...].astype(F32)
        out_ref[...] = (total_ref[...].astype(F32) + own).astype(BF16)

    return pl.pallas_call(
        kernel,
        out_shape=jax.ShapeDtypeStruct(total.shape, BF16),
        in_specs=[smem(), vmem(), vmem()],
        out_specs=vmem(),
        compiler_params=params(),
        cost_estimate=cost(total.size, 6 * total.size),
        name="added",
    )(here, total, parts)


def ring_terms(here, parts, axis):
    n = parts.shape[0]
    raising = [(i, (i + 1) % n) for i in range(n)]
    lowering = [(i, (i - 1) % n) for i in range(n)]
    hops = n // 2
    first = 2 * hops + 1 - n
    below = picked(here, parts, hops)
    below, parts = lax.optimization_barrier((below, parts))
    above = picked(here, parts, (first - hops) % n)
    above, parts = lax.optimization_barrier((above, parts))
    parts, own = staged(here, parts)
    for step in range(hops):
        if step > 0:
            below = added(here, below, parts, hops - step)
        below = lax.ppermute(below, axis, raising)
        if step > first:
            above = added(here, above, parts, (step - hops) % n)
        if step >= first:
            above = lax.ppermute(above, axis, lowering)
    return below, above, own


def local(grads, slot_block):
    replicas = lax.axis_size("dp")
    here, slot = lax.axis_index("dp")[None], lax.axis_index("fsdp")[None]
    core = slot % 2
    chips = slot_block.shape[1] // 2
    same_core = [[2 * p + c for p in range(chips)] for c in range(2)]
    across = [(i, i ^ 1) for i in range(2 * chips)]

    def exchanged(x):
        return lax.all_to_all(
            x, "fsdp", split_axis=0, concat_axis=0, axis_index_groups=same_core, tiled=True
        )

    first, second, mode = assigned(here, slot, slot_block)
    terms = ring_terms(here, grads[0], "dp")
    _, row_blocks, cols = terms[0].shape
    mine = exchanged(outgoing_pieces(first, second, terms))
    other = lax.ppermute(mine, "fsdp", across)
    right, update = first_work(core, mine, other, replicas)
    returned = exchanged(update)
    roots = slot_work(mode, core, mine, other, right, replicas)
    result = incoming_update(first, returned, row_blocks, cols // BLK)
    return result[None], roots[None, None]


def solution(mesh):
    return jax.shard_map(
        local,
        mesh=mesh,
        in_specs=(P("dp", None, "fsdp", None, None), P()),
        out_specs=(P("dp", "fsdp", None, None), P("dp", "fsdp", None, None, None)),
        check_vma=False,
    )
```

```python
import jax
import jax.numpy as jnp
from jax import lax
from jax.experimental import pallas as pl
from jax.experimental.pallas import tpu as pltpu
from jax.sharding import PartitionSpec as P

BLK = 512
LANES = 128
PER_BLK = BLK // LANES
STRIP = 64
ITERS = 2
DAMPING = 0.1
F32 = jnp.float32
BF16 = jnp.bfloat16
VMEM_LIMIT = 24 * 1024 * 1024
PICK_LIMIT = 53 * 1024 * 1024
STAGE_LIMIT = 50 * 1024 * 1024


def cost(flops, nbytes):
    return pl.CostEstimate(flops=flops, bytes_accessed=nbytes, transcendentals=0)


def vmem():
    return pl.BlockSpec(memory_space=pltpu.VMEM)


def smem():
    return pl.BlockSpec(memory_space=pltpu.SMEM)


def params(limit=VMEM_LIMIT):
    return pltpu.CompilerParams(vmem_limit_bytes=limit)


def assigned(here, slot, slot_block):
    chips = slot_block.shape[1] // 2

    def kernel(here_ref, slot_ref, table_ref, first_ref, second_ref, mode_ref, spare):
        row = here_ref[0]

        def collect(p, count):
            low, high = table_ref[row, 2 * p], table_ref[row, 2 * p + 1]
            two = jnp.logical_and(low < chips, high < chips)
            first_ref[p] = jnp.minimum(jnp.where(low < chips, low, high), chips)
            second_ref[p] = jnp.where(two, high, chips)
            spare[count] = high
            return count + two.astype(jnp.int32)

        def fill(p, count):
            empty = first_ref[p] == chips
            first_ref[p] = jnp.where(empty, spare[count], first_ref[p])
            return count + empty.astype(jnp.int32)

        lax.fori_loop(0, chips, collect, jnp.int32(0))
        lax.fori_loop(0, chips, fill, jnp.int32(0))
        kept = table_ref[row, slot_ref[0]]
        same = kept == first_ref[lax.div(slot_ref[0], 2)]
        mode_ref[0] = jnp.where(kept < chips, jnp.where(same, 1, 2), 0)

    return pl.pallas_call(
        kernel,
        out_shape=[jax.ShapeDtypeStruct((n,), jnp.int32) for n in (chips, chips, 1)],
        in_specs=[smem(), smem(), smem()],
        out_specs=[smem(), smem(), smem()],
        scratch_shapes=[pltpu.SMEM((chips + 1,), jnp.int32)],
        compiler_params=params(),
        cost_estimate=cost(0, 1024),
        name="assigned",
    )(here, slot, slot_block)


def outgoing_pieces(first, second, terms):
    rows, row_blocks, cols = terms[0].shape
    col_blocks = cols // BLK
    group = row_blocks * col_blocks
    chips = first.shape[0]

    def kernel(
        first_ref, second_ref, below_ref, above_ref, own_ref, out_ref, wide, pieces
    ):
        for k in range(cols // LANES):
            at = (slice(None), slice(None), slice(k * LANES, (k + 1) * LANES))
            lanes = below_ref[at].astype(F32) + above_ref[at].astype(F32)
            lanes = lanes + own_ref[at].astype(F32)
            wide[k] = lanes.reshape(rows * row_blocks, LANES)
        for rb in range(row_blocks):
            for k in range(cols // LANES):
                v, at = rb * col_blocks + k // PER_BLK, k % PER_BLK * LANES
                part = wide[k, pl.ds(rb, rows, stride=row_blocks), :]
                pieces[v, :, at : at + LANES] = part.astype(BF16)
        pieces[group] = jnp.zeros((rows, BLK), BF16)

        def place(p, carry):
            out_ref[p, 0] = pieces[first_ref[p]]
            out_ref[p, 1] = pieces[second_ref[p]]
            return carry

        lax.fori_loop(0, chips, place, 0, unroll=4)

    return pl.pallas_call(
        kernel,
        out_shape=jax.ShapeDtypeStruct((chips, 2, rows, BLK), BF16),
        in_specs=[smem(), smem(), vmem(), vmem(), vmem()],
        out_specs=vmem(),
        scratch_shapes=[
            pltpu.VMEM((cols // LANES, rows * row_blocks, LANES), F32),
            pltpu.VMEM((group + 1, rows, BLK), BF16),
        ],
        compiler_params=params(),
        cost_estimate=cost(0, 6 * chips * rows * BLK * 2),
        name="outgoing",
    )(first, second, *terms)


def incoming_update(first, returned, row_blocks, col_blocks):
    chips, rows, _ = returned.shape
    cols = col_blocks * BLK

    def kernel(first_ref, x_ref, out_ref, wide, pieces):
        def place(s, carry):
            pieces[first_ref[s]] = x_ref[s]
            return carry

        lax.fori_loop(0, chips, place, 0, unroll=4)
        for rb in range(row_blocks):
            for k in range(cols // LANES):
                v, at = rb * col_blocks + k // PER_BLK, k % PER_BLK * LANES
                part = pieces[v, :, at : at + LANES].astype(F32)
                wide[k, pl.ds(rb, rows, stride=row_blocks), :] = part
        for k in range(cols // LANES):
            lanes = wide[k].reshape(rows, row_blocks, LANES)
            out_ref[:, :, k * LANES : (k + 1) * LANES] = lanes.astype(BF16)

    return pl.pallas_call(
        kernel,
        out_shape=jax.ShapeDtypeStruct((rows, row_blocks, cols), BF16),
        in_specs=[smem(), vmem()],
        out_specs=vmem(),
        scratch_shapes=[
            pltpu.VMEM((cols // LANES, rows * row_blocks, LANES), F32),
            pltpu.VMEM((chips, rows, BLK), BF16),
        ],
        compiler_params=params(),
        cost_estimate=cost(0, 3 * chips * rows * BLK * 2),
        name="incoming",
    )(first, returned)


def dot(a, b, contract=((1,), (0,))):
    return lax.dot_general(a, b, (contract, ((), ())), preferred_element_type=F32)


def strips(rows=BLK):
    return [slice(at, at + STRIP) for at in range(0, rows, STRIP)]


def folded(x):
    return jnp.sum(x.reshape(-1, 8, x.shape[-1]), axis=0)


def put_linear(out_ref, in_ref, times, diagonal):
    row = lax.broadcasted_iota(jnp.int32, (STRIP, LANES), 0)
    lane = lax.broadcasted_iota(jnp.int32, (STRIP, LANES), 1)
    for at in strips():
        x = in_ref[at, :] * times
        out_ref[at, :] = x.astype(BF16)
        left = at.start // LANES * LANES
        lanes = slice(left, left + LANES)
        eye = jnp.where(row + (at.start - left) == lane, diagonal, 0.0)
        out_ref[at, lanes] = (x[:, lanes] + eye).astype(BF16)


def newton_root(gram, total, scale, low, rest, root):
    shift = DAMPING * total / BLK + 1e-06
    squares = sum(folded(gram[at, :] * gram[at, :]) for at in strips())
    squares = jnp.sum(squares) * (scale * scale)
    norm = jnp.sqrt(squares + 2.0 * shift * total + BLK * shift * shift) / 4.0
    times, diagonal = scale / norm, shift / norm
    start = lax.rsqrt(jnp.sqrt(norm))
    for iteration in range(ITERS):
        put_linear(low, gram, -0.25 * times, 1.25 - 0.25 * diagonal)
        if iteration == 0:
            put_linear(root, gram, -0.25 * times * start, (1.25 - 0.25 * diagonal) * start)
        else:
            root[...] = dot(root[...], low[...]).astype(BF16)
        if iteration + 1 < ITERS:
            put_linear(rest, gram, times, diagonal)
            square = dot(low[...], low[...]).astype(BF16)
            fourth = dot(square, square).astype(BF16)
            gram[...] = dot(fourth, rest[...])
            times, diagonal = 1.0, 0.0


def whole_block(core_ref, mine_ref, other_ref, which, halves, block):
    halves[:, core_ref[0]] = mine_ref[:, which].astype(F32)
    halves[:, 1 - core_ref[0]] = other_ref[:, which].astype(F32)
    chips, _, rows, _ = halves.shape
    per_strip = STRIP // (2 * rows)
    squares = 0.0
    for k, at in enumerate(strips()):
        x = halves[k * per_strip : (k + 1) * per_strip].reshape(STRIP, BLK)
        block[at, :] = x.astype(BF16)
        squares += folded(x * x)
    return jnp.sum(squares)


def buffers(chips, rows):
    return [
        pltpu.VMEM((chips, 2, rows, BLK), F32),
        pltpu.VMEM((BLK, BLK), F32),
        pltpu.VMEM((BLK, BLK), BF16),
        pltpu.VMEM((BLK, BLK), BF16),
        pltpu.VMEM((BLK, BLK), BF16),
    ]


def first_work(core, mine, other, replicas):
    chips, _, rows, _ = mine.shape
    scale = 1.0 / (replicas * replicas)

    def kernel(core_ref, mine_ref, other_ref, right, update_ref, halves, gram, block, low, rest):
        total = whole_block(core_ref, mine_ref, other_ref, 0, halves, block) * scale
        gram[...] = dot(block[...], block[...], ((0,), (0,)))
        newton_root(gram, total, scale, low, rest, right)
        low[...] = (dot(block[...], right[...]) * (1.0 / replicas)).astype(BF16)
        halves[...] = dot(low[...], right[...]).reshape(halves.shape)
        squares = sum(folded(halves[p] * halves[p]) for p in range(chips))
        count = BLK * BLK
        grad_rms = jnp.sqrt(total / count)
        dir_rms = jnp.sqrt(jnp.sum(squares) / count + 1e-06)
        factor = -(grad_rms / dir_rms)
        for p in range(0, chips, 4):
            update_ref[p : p + 4] = (halves[p : p + 4, core_ref[0]] * factor).astype(BF16)

    return pl.pallas_call(
        kernel,
        out_shape=(
            jax.ShapeDtypeStruct((BLK, BLK), BF16),
            jax.ShapeDtypeStruct((chips, rows, BLK), BF16),
        ),
        in_specs=[smem(), vmem(), vmem()],
        out_specs=(vmem(), vmem()),
        scratch_shapes=buffers(chips, rows),
        compiler_params=params(),
        cost_estimate=cost(14 * BLK**3, 8 * BLK * BLK),
        name="first_work",
    )(core, mine, other)


def slot_work(mode, core, mine, other, first_right, replicas):
    chips, _, rows, _ = mine.shape
    scale = 1.0 / (replicas * replicas)

    def kernel(mode_ref, core_ref, mine_ref, other_ref, right_ref, out_ref, halves, gram, block, low, rest):
        def left_root(which):
            total = whole_block(core_ref, mine_ref, other_ref, which, halves, block) * scale
            gram[...] = dot(block[...], block[...], ((1,), (1,)))
            newton_root(gram, total, scale, low, rest, out_ref.at[0])
            return total

        @pl.when(mode_ref[0] == 0)
        def _():
            out_ref[...] = jnp.zeros_like(out_ref)

        @pl.when(mode_ref[0] == 1)
        def _():
            left_root(0)
            out_ref[1] = right_ref[...]

        @pl.when(mode_ref[0] == 2)
        def _():
            total = left_root(1)
            gram[...] = dot(block[...], block[...], ((0,), (0,)))
            newton_root(gram, total, scale, low, rest, out_ref.at[1])

    return pl.pallas_call(
        kernel,
        out_shape=jax.ShapeDtypeStruct((2, BLK, BLK), BF16),
        in_specs=[smem(), smem(), vmem(), vmem(), vmem()],
        out_specs=vmem(),
        scratch_shapes=buffers(chips, rows),
        compiler_params=params(),
        cost_estimate=cost(20 * BLK**3, 8 * BLK * BLK),
        name="slot_work",
    )(mode, core, mine, other, first_right)


def part_of(parts_ref, here_ref, offset):
    return parts_ref.at[lax.rem(here_ref[0] + offset, parts_ref.shape[0])]


def picked(here, parts, offset):
    def kernel(here_ref, parts_ref, out_ref, sem):
        copy = pltpu.make_async_copy(part_of(parts_ref, here_ref, offset), out_ref, sem.at[0])
        copy.start()
        copy.wait()

    return pl.pallas_call(
        kernel,
        out_shape=jax.ShapeDtypeStruct(parts.shape[1:], BF16),
        in_specs=[smem(), pl.BlockSpec(memory_space=pltpu.HBM)],
        out_specs=vmem(),
        scratch_shapes=[pltpu.SemaphoreType.DMA((1,))],
        compiler_params=params(PICK_LIMIT),
        cost_estimate=cost(0, 4 * parts[0].size),
        name="picked",
    )(here, parts)


def staged(here, parts):
    def kernel(here_ref, parts_ref, all_ref, own_ref, sems):
        copies = [
            pltpu.make_async_copy(parts_ref, all_ref, sems.at[0]),
            pltpu.make_async_copy(part_of(parts_ref, here_ref, 0), own_ref, sems.at[1]),
        ]
        for copy in copies:
            copy.start()
        for copy in copies:
            copy.wait()

    return pl.pallas_call(
        kernel,
        out_shape=[
            jax.ShapeDtypeStruct(parts.shape, BF16),
            jax.ShapeDtypeStruct(parts.shape[1:], BF16),
        ],
        in_specs=[smem(), pl.BlockSpec(memory_space=pltpu.HBM)],
        out_specs=[vmem(), vmem()],
        scratch_shapes=[pltpu.SemaphoreType.DMA((2,))],
        compiler_params=params(STAGE_LIMIT),
        cost_estimate=cost(0, 4 * parts.size),
        name="staged",
    )(here, parts)


def added(here, total, parts, offset):
    def kernel(here_ref, total_ref, parts_ref, out_ref):
        own = part_of(parts_ref, here_ref, offset)[...].astype(F32)
        out_ref[...] = (total_ref[...].astype(F32) + own).astype(BF16)

    return pl.pallas_call(
        kernel,
        out_shape=jax.ShapeDtypeStruct(total.shape, BF16),
        in_specs=[smem(), vmem(), vmem()],
        out_specs=vmem(),
        compiler_params=params(),
        cost_estimate=cost(total.size, 6 * total.size),
        name="added",
    )(here, total, parts)


def ring_terms(here, parts, axis):
    n = parts.shape[0]
    raising = [(i, (i + 1) % n) for i in range(n)]
    lowering = [(i, (i - 1) % n) for i in range(n)]
    hops = n // 2
    first = 2 * hops + 1 - n
    below = picked(here, parts, hops)
    below, parts = lax.optimization_barrier((below, parts))
    above = picked(here, parts, (first - hops) % n)
    above, parts = lax.optimization_barrier((above, parts))
    parts, own = staged(here, parts)
    for step in range(hops):
        if step > 0:
            below = added(here, below, parts, hops - step)
        below = lax.ppermute(below, axis, raising)
        if step > first:
            above = added(here, above, parts, (step - hops) % n)
        if step >= first:
            above = lax.ppermute(above, axis, lowering)
    return below, above, own


def local(grads, slot_block):
    replicas = lax.axis_size("dp")
    here, slot = lax.axis_index("dp")[None], lax.axis_index("fsdp")[None]
    core = slot % 2
    chips = slot_block.shape[1] // 2
    same_core = [[2 * p + c for p in range(chips)] for c in range(2)]
    across = [(i, i ^ 1) for i in range(2 * chips)]

    def exchanged(x):
        return lax.all_to_all(
            x, "fsdp", split_axis=0, concat_axis=0, axis_index_groups=same_core, tiled=True
        )

    first, second, mode = assigned(here, slot, slot_block)
    terms = ring_terms(here, grads[0], "dp")
    _, row_blocks, cols = terms[0].shape
    mine = exchanged(outgoing_pieces(first, second, terms))
    other = lax.ppermute(mine, "fsdp", across)
    right, update = first_work(core, mine, other, replicas)
    returned = exchanged(update)
    roots = slot_work(mode, core, mine, other, right, replicas)
    result = incoming_update(first, returned, row_blocks, cols // BLK)
    return result[None], roots[None, None]


def solution(mesh):
    return jax.shard_map(
        local,
        mesh=mesh,
        in_specs=(P("dp", None, "fsdp", None, None), P()),
        out_specs=(P("dp", "fsdp", None, None), P("dp", "fsdp", None, None, None)),
        check_vma=False,
    )
```

```python
import jax
import jax.numpy as jnp
from jax import lax
from jax.experimental import pallas as pl
from jax.experimental.pallas import tpu as pltpu
from jax.sharding import PartitionSpec as P

BLK = 512
LANES = 128
PER_BLK = BLK // LANES
STRIP = 64
ITERS = 2
DAMPING = 0.1
F32 = jnp.float32
BF16 = jnp.bfloat16
VMEM_LIMIT = 24 * 1024 * 1024
PICK_LIMIT = 53 * 1024 * 1024
STAGE_LIMIT = 50 * 1024 * 1024


def cost(flops, nbytes):
    return pl.CostEstimate(flops=flops, bytes_accessed=nbytes, transcendentals=0)


def vmem():
    return pl.BlockSpec(memory_space=pltpu.VMEM)


def smem():
    return pl.BlockSpec(memory_space=pltpu.SMEM)


def params(limit=VMEM_LIMIT):
    return pltpu.CompilerParams(vmem_limit_bytes=limit)


def assigned(here, slot, slot_block):
    chips = slot_block.shape[1] // 2

    def kernel(here_ref, slot_ref, table_ref, first_ref, second_ref, mode_ref, spare):
        row = here_ref[0]

        def collect(p, count):
            low, high = table_ref[row, 2 * p], table_ref[row, 2 * p + 1]
            two = jnp.logical_and(low < chips, high < chips)
            first_ref[p] = jnp.minimum(jnp.where(low < chips, low, high), chips)
            second_ref[p] = jnp.where(two, high, chips)
            spare[count] = high
            return count + two.astype(jnp.int32)

        def fill(p, count):
            empty = first_ref[p] == chips
            first_ref[p] = jnp.where(empty, spare[count], first_ref[p])
            return count + empty.astype(jnp.int32)

        lax.fori_loop(0, chips, collect, jnp.int32(0))
        lax.fori_loop(0, chips, fill, jnp.int32(0))
        kept = table_ref[row, slot_ref[0]]
        same = kept == first_ref[lax.div(slot_ref[0], 2)]
        mode_ref[0] = jnp.where(kept < chips, jnp.where(same, 1, 2), 0)

    return pl.pallas_call(
        kernel,
        out_shape=[jax.ShapeDtypeStruct((n,), jnp.int32) for n in (chips, chips, 1)],
        in_specs=[smem(), smem(), smem()],
        out_specs=[smem(), smem(), smem()],
        scratch_shapes=[pltpu.SMEM((chips + 1,), jnp.int32)],
        compiler_params=params(),
        cost_estimate=cost(0, 1024),
        name="assigned",
    )(here, slot, slot_block)


def outgoing_pieces(first, second, terms):
    rows, row_blocks, cols = terms[0].shape
    col_blocks = cols // BLK
    group = row_blocks * col_blocks
    chips = first.shape[0]

    def kernel(
        first_ref, second_ref, below_ref, above_ref, own_ref, out_ref, wide, pieces
    ):
        for k in range(cols // LANES):
            at = (slice(None), slice(None), slice(k * LANES, (k + 1) * LANES))
            lanes = below_ref[at].astype(F32) + above_ref[at].astype(F32)
            lanes = lanes + own_ref[at].astype(F32)
            wide[k] = lanes.reshape(rows * row_blocks, LANES)
        for rb in range(row_blocks):
            for k in range(cols // LANES):
                v, at = rb * col_blocks + k // PER_BLK, k % PER_BLK * LANES
                part = wide[k, pl.ds(rb, rows, stride=row_blocks), :]
                pieces[v, :, at : at + LANES] = part.astype(BF16)
        pieces[group] = jnp.zeros((rows, BLK), BF16)

        def place(p, carry):
            out_ref[p, 0] = pieces[first_ref[p]]
            out_ref[p, 1] = pieces[second_ref[p]]
            return carry

        lax.fori_loop(0, chips, place, 0, unroll=4)

    return pl.pallas_call(
        kernel,
        out_shape=jax.ShapeDtypeStruct((chips, 2, rows, BLK), BF16),
        in_specs=[smem(), smem(), vmem(), vmem(), vmem()],
        out_specs=vmem(),
        scratch_shapes=[
            pltpu.VMEM((cols // LANES, rows * row_blocks, LANES), F32),
            pltpu.VMEM((group + 1, rows, BLK), BF16),
        ],
        compiler_params=params(),
        cost_estimate=cost(0, 6 * chips * rows * BLK * 2),
        name="outgoing",
    )(first, second, *terms)


def incoming_update(first, returned, row_blocks, col_blocks):
    chips, rows, _ = returned.shape
    cols = col_blocks * BLK

    def kernel(first_ref, x_ref, out_ref, wide, pieces):
        def place(s, carry):
            pieces[first_ref[s]] = x_ref[s]
            return carry

        lax.fori_loop(0, chips, place, 0, unroll=4)
        for rb in range(row_blocks):
            for k in range(cols // LANES):
                v, at = rb * col_blocks + k // PER_BLK, k % PER_BLK * LANES
                part = pieces[v, :, at : at + LANES].astype(F32)
                wide[k, pl.ds(rb, rows, stride=row_blocks), :] = part
        for k in range(cols // LANES):
            lanes = wide[k].reshape(rows, row_blocks, LANES)
            out_ref[:, :, k * LANES : (k + 1) * LANES] = lanes.astype(BF16)

    return pl.pallas_call(
        kernel,
        out_shape=jax.ShapeDtypeStruct((rows, row_blocks, cols), BF16),
        in_specs=[smem(), vmem()],
        out_specs=vmem(),
        scratch_shapes=[
            pltpu.VMEM((cols // LANES, rows * row_blocks, LANES), F32),
            pltpu.VMEM((chips, rows, BLK), BF16),
        ],
        compiler_params=params(),
        cost_estimate=cost(0, 3 * chips * rows * BLK * 2),
        name="incoming",
    )(first, returned)


def dot(a, b, contract=((1,), (0,))):
    return lax.dot_general(a, b, (contract, ((), ())), preferred_element_type=F32)


def strips(rows=BLK):
    return [slice(at, at + STRIP) for at in range(0, rows, STRIP)]


def folded(x):
    return jnp.sum(x.reshape(-1, 8, x.shape[-1]), axis=0)


def put_linear(out_ref, in_ref, times, diagonal):
    row = lax.broadcasted_iota(jnp.int32, (STRIP, LANES), 0)
    lane = lax.broadcasted_iota(jnp.int32, (STRIP, LANES), 1)
    for at in strips():
        x = in_ref[at, :] * times
        out_ref[at, :] = x.astype(BF16)
        left = at.start // LANES * LANES
        lanes = slice(left, left + LANES)
        eye = jnp.where(row + (at.start - left) == lane, diagonal, 0.0)
        out_ref[at, lanes] = (x[:, lanes] + eye).astype(BF16)


def newton_root(gram, total, scale, low, rest, root):
    shift = DAMPING * total / BLK + 1e-06
    squares = sum(folded(gram[at, :] * gram[at, :]) for at in strips())
    squares = jnp.sum(squares) * (scale * scale)
    norm = jnp.sqrt(squares + 2.0 * shift * total + BLK * shift * shift) / 4.0
    times, diagonal = scale / norm, shift / norm
    start = lax.rsqrt(jnp.sqrt(norm))
    for iteration in range(ITERS):
        put_linear(low, gram, -0.25 * times, 1.25 - 0.25 * diagonal)
        if iteration == 0:
            put_linear(root, gram, -0.25 * times * start, (1.25 - 0.25 * diagonal) * start)
        else:
            root[...] = dot(root[...], low[...]).astype(BF16)
        if iteration + 1 < ITERS:
            put_linear(rest, gram, times, diagonal)
            square = dot(low[...], low[...]).astype(BF16)
            fourth = dot(square, square).astype(BF16)
            gram[...] = dot(fourth, rest[...])
            times, diagonal = 1.0, 0.0


def whole_block(core_ref, mine_ref, other_ref, which, halves, block):
    halves[:, core_ref[0]] = mine_ref[:, which].astype(F32)
    halves[:, 1 - core_ref[0]] = other_ref[:, which].astype(F32)
    chips, _, rows, _ = halves.shape
    per_strip = STRIP // (2 * rows)
    squares = 0.0
    for k, at in enumerate(strips()):
        x = halves[k * per_strip : (k + 1) * per_strip].reshape(STRIP, BLK)
        block[at, :] = x.astype(BF16)
        squares += folded(x * x)
    return jnp.sum(squares)


def buffers(chips, rows):
    return [
        pltpu.VMEM((chips, 2, rows, BLK), F32),
        pltpu.VMEM((BLK, BLK), F32),
        pltpu.VMEM((BLK, BLK), BF16),
        pltpu.VMEM((BLK, BLK), BF16),
        pltpu.VMEM((BLK, BLK), BF16),
    ]


def first_work(core, mine, other, replicas):
    chips, _, rows, _ = mine.shape
    scale = 1.0 / (replicas * replicas)

    def kernel(core_ref, mine_ref, other_ref, right, update_ref, halves, gram, block, low, rest):
        total = whole_block(core_ref, mine_ref, other_ref, 0, halves, block) * scale
        gram[...] = dot(block[...], block[...], ((0,), (0,)))
        newton_root(gram, total, scale, low, rest, right)
        low[...] = (dot(block[...], right[...]) * (1.0 / replicas)).astype(BF16)
        halves[...] = dot(low[...], right[...]).reshape(halves.shape)
        squares = sum(folded(halves[p] * halves[p]) for p in range(chips))
        count = BLK * BLK
        grad_rms = jnp.sqrt(total / count)
        dir_rms = jnp.sqrt(jnp.sum(squares) / count + 1e-06)
        factor = -(grad_rms / dir_rms)
        for p in range(0, chips, 4):
            update_ref[p : p + 4] = (halves[p : p + 4, core_ref[0]] * factor).astype(BF16)

    return pl.pallas_call(
        kernel,
        out_shape=(
            jax.ShapeDtypeStruct((BLK, BLK), BF16),
            jax.ShapeDtypeStruct((chips, rows, BLK), BF16),
        ),
        in_specs=[smem(), vmem(), vmem()],
        out_specs=(vmem(), vmem()),
        scratch_shapes=buffers(chips, rows),
        compiler_params=params(),
        cost_estimate=cost(14 * BLK**3, 8 * BLK * BLK),
        name="first_work",
    )(core, mine, other)


def slot_work(mode, core, mine, other, first_right, replicas):
    chips, _, rows, _ = mine.shape
    scale = 1.0 / (replicas * replicas)

    def kernel(mode_ref, core_ref, mine_ref, other_ref, right_ref, out_ref, halves, gram, block, low, rest):
        def left_root(which):
            total = whole_block(core_ref, mine_ref, other_ref, which, halves, block) * scale
            gram[...] = dot(block[...], block[...], ((1,), (1,)))
            newton_root(gram, total, scale, low, rest, out_ref.at[0])
            return total

        @pl.when(mode_ref[0] == 0)
        def _():
            out_ref[...] = jnp.zeros_like(out_ref)

        @pl.when(mode_ref[0] == 1)
        def _():
            left_root(0)
            out_ref[1] = right_ref[...]

        @pl.when(mode_ref[0] == 2)
        def _():
            total = left_root(1)
            gram[...] = dot(block[...], block[...], ((0,), (0,)))
            newton_root(gram, total, scale, low, rest, out_ref.at[1])

    return pl.pallas_call(
        kernel,
        out_shape=jax.ShapeDtypeStruct((2, BLK, BLK), BF16),
        in_specs=[smem(), smem(), vmem(), vmem(), vmem()],
        out_specs=vmem(),
        scratch_shapes=buffers(chips, rows),
        compiler_params=params(),
        cost_estimate=cost(20 * BLK**3, 8 * BLK * BLK),
        name="slot_work",
    )(mode, core, mine, other, first_right)


def part_of(parts_ref, here_ref, offset):
    return parts_ref.at[lax.rem(here_ref[0] + offset, parts_ref.shape[0])]


def picked(here, parts, offset):
    def kernel(here_ref, parts_ref, out_ref, sem):
        copy = pltpu.make_async_copy(part_of(parts_ref, here_ref, offset), out_ref, sem.at[0])
        copy.start()
        copy.wait()

    return pl.pallas_call(
        kernel,
        out_shape=jax.ShapeDtypeStruct(parts.shape[1:], BF16),
        in_specs=[smem(), pl.BlockSpec(memory_space=pltpu.HBM)],
        out_specs=vmem(),
        scratch_shapes=[pltpu.SemaphoreType.DMA((1,))],
        compiler_params=params(PICK_LIMIT),
        cost_estimate=cost(0, 4 * parts[0].size),
        name="picked",
    )(here, parts)


def staged(here, parts):
    def kernel(here_ref, parts_ref, all_ref, own_ref, sems):
        copies = [
            pltpu.make_async_copy(parts_ref, all_ref, sems.at[0]),
            pltpu.make_async_copy(part_of(parts_ref, here_ref, 0), own_ref, sems.at[1]),
        ]
        for copy in copies:
            copy.start()
        for copy in copies:
            copy.wait()

    return pl.pallas_call(
        kernel,
        out_shape=[
            jax.ShapeDtypeStruct(parts.shape, BF16),
            jax.ShapeDtypeStruct(parts.shape[1:], BF16),
        ],
        in_specs=[smem(), pl.BlockSpec(memory_space=pltpu.HBM)],
        out_specs=[vmem(), vmem()],
        scratch_shapes=[pltpu.SemaphoreType.DMA((2,))],
        compiler_params=params(STAGE_LIMIT),
        cost_estimate=cost(0, 4 * parts.size),
        name="staged",
    )(here, parts)


def added(here, total, parts, offset, more=None):
    given = (total,) if more is None else (total, more)

    def kernel(here_ref, parts_ref, *refs):
        out_ref = refs[-1]
        own = part_of(parts_ref, here_ref, offset)[...].astype(F32)
        out_ref[...] = sum((x[...].astype(F32) for x in refs[:-1]), own).astype(BF16)

    return pl.pallas_call(
        kernel,
        out_shape=jax.ShapeDtypeStruct(total.shape, BF16),
        in_specs=[smem(), vmem()] + [vmem()] * len(given),
        out_specs=vmem(),
        compiler_params=params(),
        cost_estimate=cost(total.size, 6 * total.size),
        name="added",
    )(here, parts, *given)


def ring_terms(here, parts, axis):
    n = parts.shape[0]
    raising = [(i, (i + 1) % n) for i in range(n)]
    lowering = [(i, (i - 1) % n) for i in range(n)]
    hops = n // 2
    first = 2 * hops + 1 - n
    skipping = [(i, (i + 2) % n) for i in range(n)]
    near = picked(here, parts, hops - 1)
    near, parts = lax.optimization_barrier((near, parts))
    far, above = picked(here, parts, hops), picked(here, parts, (first - hops) % n)
    far, above, parts = lax.optimization_barrier((far, above, parts))
    parts, own = staged(here, parts)
    near = lax.ppermute(near, axis, raising)
    far = lax.ppermute(far, axis, skipping)
    below = added(here, near, parts, hops - 2, far)
    for step in range(first, hops):
        if step > first:
            above = added(here, above, parts, (step - hops) % n)
        above = lax.ppermute(above, axis, lowering)
        if step > first:
            if step > first + 1:
                below = added(here, below, parts, hops - step)
            below = lax.ppermute(below, axis, raising)
    return below, above, own


def local(grads, slot_block):
    replicas = lax.axis_size("dp")
    here, slot = lax.axis_index("dp")[None], lax.axis_index("fsdp")[None]
    core = slot % 2
    chips = slot_block.shape[1] // 2
    same_core = [[2 * p + c for p in range(chips)] for c in range(2)]
    across = [(i, i ^ 1) for i in range(2 * chips)]

    def exchanged(x):
        return lax.all_to_all(
            x, "fsdp", split_axis=0, concat_axis=0, axis_index_groups=same_core, tiled=True
        )

    first, second, mode = assigned(here, slot, slot_block)
    terms = ring_terms(here, grads[0], "dp")
    _, row_blocks, cols = terms[0].shape
    mine = exchanged(outgoing_pieces(first, second, terms))
    other = lax.ppermute(mine, "fsdp", across)
    right, update = first_work(core, mine, other, replicas)
    returned = exchanged(update)
    roots = slot_work(mode, core, mine, other, right, replicas)
    result = incoming_update(first, returned, row_blocks, cols // BLK)
    return result[None], roots[None, None]


def solution(mesh):
    return jax.shard_map(
        local,
        mesh=mesh,
        in_specs=(P("dp", None, "fsdp", None, None), P()),
        out_specs=(P("dp", "fsdp", None, None), P("dp", "fsdp", None, None, None)),
        check_vma=False,
    )
```
